128 devices in a mesh: tm: 4 (over y_lo, core), height: 32 (over y_hi, z, x).
Axes of the slice: x: 4, y: 4 (y_hi: 2, y_lo: 2; y = y_hi * 2 + y_lo), z: 4, core: 2. Of those that a mesh axis runs over, the one named last changes fastest.
Arguments:
- latents: bfloat16 [8, 64, 640, 384], P('tm', 'height'), may hold values from -6 to 6
- cotangent: bfloat16 [8, 64, 640, 384], P('tm', 'height'), may hold values from -6 to 6
- temporal_weight: bfloat16 [3, 384, 384], replicated, may hold values from -0.1875 to 0.1875
- spatial_weight: bfloat16 [3, 3, 384, 384], replicated, may hold values from -0.109375 to 0.109375
Outputs:
- latent_grad: bfloat16 [8, 64, 640, 384], P('tm', 'height')
- temporal_grad: float32 [3, 384, 384], replicated
- spatial_grad: float32 [3, 3, 384, 384], replicated
The draws below stay inside these ranges and needn't reach their ends.
All inputs are finite; a program needn't handle non-finite values.
Results may differ from the reference program's by a relative error of at most 0.0054.
Values may be sent and summed in bfloat16 or wider, within the bound.
A program may use at most 128 MiB of HBM per device.

```python
import jax
import jax.numpy as jnp

C = 384
WIDTH = 640
FRAMES = 8
ROWS = 64


def levels(rng, extent, shards, least, high):
    def one(dim, shards_of):
        steps = jax.random.uniform(jax.random.fold_in(jax.random.fold_in(rng, 6), dim), (shards_of,), jnp.float32, least / len(shards), high / len(shards))
        return jnp.repeat(jnp.exp(steps), extent[dim] // shards_of).reshape((-1,) + (1,) * (len(extent) - dim - 1))

    gain = one(*shards[0])
    for cut in shards[1:]:
        gain = gain * one(*cut)
    return gain


def noise(rng, extent, width, most, shards=(), kind=jnp.bfloat16):
    drawn = jax.random.normal(rng, extent, jnp.float32) * width
    if len(shards) > 0:
        drawn = levels(rng, extent, shards, -0.22, 0.18) * drawn
    return jnp.clip(drawn, min=-most, max=most).astype(kind)


def setup_inputs(seed: int = 0) -> dict:
    key_list = jax.random.split(jax.random.key(seed), 5)
    return {
        "latents": noise(key_list[0], (FRAMES, ROWS, WIDTH, C), 1.0, 6.0, ((0, 4), (1, 32))),
        "cotangent": noise(key_list[1], (FRAMES, ROWS, WIDTH, C), 1.0, 6.0, ((0, 4), (1, 32))),
        "temporal_weight": noise(key_list[2], (3, C, C), (3 * C) ** -0.5, 0.1875),
        "spatial_weight": noise(key_list[3], (3, 3, C, C), (9 * C) ** -0.5, 0.109375),
    }


def flat(value):
    return value.reshape(-1, value.shape[-1])


def moved(value, step_rows, step_cols):
    rows, cols = value.shape[1], value.shape[2]
    padded = jnp.pad(value, ((0, 0), (1, 1), (1, 1), (0, 0)))
    return padded[:, 1 - step_rows:1 - step_rows + rows, 1 - step_cols:1 - step_cols + cols]


def reference(latents, cotangent, temporal_weight, spatial_weight):
    frames, rows, cols, chans = latents.shape
    scale = 1.0 / (frames * rows * cols) ** 0.5
    before = jnp.concatenate([jnp.zeros((2, rows, cols, chans), jnp.bfloat16), latents], axis=0)
    pre = jnp.zeros((frames * rows * cols, chans), jnp.float32)
    for tap in range(3):
        pre = pre + jnp.dot(flat(before[2 - tap:2 - tap + frames]), temporal_weight[tap], preferred_element_type=jnp.float32)
    hidden = jax.nn.silu(pre).astype(jnp.bfloat16)
    back = jnp.zeros((frames * rows * cols, chans), jnp.float32)
    spatial = []
    for i in range(3):
        for j in range(3):
            window = flat(moved(cotangent, i - 1, j - 1))
            back = back + jnp.dot(window, spatial_weight[i, j].T, preferred_element_type=jnp.float32)
            spatial.append(jnp.dot(hidden.T, window, preferred_element_type=jnp.float32))
    sigma = jax.nn.sigmoid(pre)
    pre_grad = (back * sigma * (1.0 + pre * (1.0 - sigma))).astype(jnp.bfloat16)
    grid = pre_grad.reshape(frames, rows, cols, chans)
    after = jnp.concatenate([grid, jnp.zeros((2, rows, cols, chans), jnp.bfloat16)], axis=0)
    total = flat(cotangent).astype(jnp.float32)
    temporal = []
    for tap in range(3):
        total = total + jnp.dot(flat(after[tap:tap + frames]), temporal_weight[tap].T, preferred_element_type=jnp.float32)
        temporal.append(jnp.dot(flat(before[2 - tap:2 - tap + frames]).T, pre_grad, preferred_element_type=jnp.float32))
    latent_grad = total.reshape(frames, rows, cols, chans).astype(jnp.bfloat16)
    temporal_grad = jnp.stack(temporal) * scale
    spatial_grad = jnp.stack(spatial).reshape(3, 3, chans, chans) * scale
    return latent_grad, temporal_grad, spatial_grad
```

```python
import math

import jax
import jax.numpy as jnp
from jax import lax
from jax.experimental import pallas as pl
from jax.experimental.pallas import tpu as pltpu
from jax.sharding import PartitionSpec as P

BF = jnp.bfloat16
F32 = jnp.float32
MESH = pl.DeviceIdType.MESH
HALF = 192
QUART = 48


class Place:
    def __init__(self):
        tm = lax.axis_index("tm")
        height = lax.axis_index("height")
        self.tm = tm
        self.height = height
        self.core = tm % 2
        self.xyz = (height % 4, (height // 16) * 2 + tm // 2, (height // 4) % 4)

    def at(self, x, y, z, core):
        return ((y % 2) * 2 + core, (y // 2) * 16 + z * 4 + x)

    def along(self, axis, where):
        xyz = list(self.xyz)
        xyz[axis] = where
        return self.at(*xyz, self.core)

    def other(self):
        return (self.tm + 1 - 2 * self.core, self.height)


def remote(src, dst, send, recv, device):
    return pltpu.make_async_remote_copy(
        src_ref=src, dst_ref=dst, send_sem=send, recv_sem=recv,
        device_id=device, device_id_type=MESH)


class Reduce:
    SCRATCH = [
        pltpu.VMEM((12, HALF, 384), BF),
        pltpu.VMEM((12, HALF, 384), BF),
        pltpu.VMEM((12, HALF, 384), BF),
        pltpu.VMEM((12, QUART, 384), F32),
        pltpu.VMEM((12, 3, QUART, 384), BF),
        pltpu.VMEM((12, QUART, 384), BF),
        pltpu.VMEM((3, 3, QUART, 384), BF),
        pltpu.VMEM((3, 4, QUART, 384), BF),
        pltpu.SemaphoreType.DMA((12, 2)),
        pltpu.SemaphoreType.DMA((12, 3, 2)),
        pltpu.SemaphoreType.DMA((12,)),
        pltpu.SemaphoreType.DMA((3, 3)),
        pltpu.SemaphoreType.DMA((3, 3, 2)),
        pltpu.SemaphoreType.DMA((3, 3)),
        pltpu.SemaphoreType.DMA((12,)),
        pltpu.SemaphoreType.DMA((12, 3, 2)),
        pltpu.SemaphoreType.DMA((12, 2)),
    ]

    def __init__(self, place, part, out, refs):
        self.place = place
        self.part = part
        self.out = out
        (self.c_out, self.c_in, self.q_out, self.q_own, self.q_in, self.s_out, self.s_in, self.t_buf,
         self.c_sem, self.q_sem, self.s_send, self.s_recv, self.t_sem, self.g2_send, self.g2_recv,
         self.g1_sem, self.gc_sem) = refs

    def core_copy(self, t):
        return remote(self.c_out.at[t], self.c_in.at[t], self.c_sem.at[t, 0], self.c_sem.at[t, 1], self.place.other())

    def quarter_copy(self, t, o, d):
        q = (self.place.xyz[o] + d) % 4
        return remote(self.q_out.at[t, pl.ds(q * QUART, QUART)], self.q_in.at[t, d - 1],
                      self.q_sem.at[t, d - 1, 0], self.q_sem.at[t, d - 1, 1], self.place.along(o, q))

    def second_copy(self, t, o, g, slot):
        b = (o + 1) % 3
        return remote(self.s_out.at[t], self.s_in.at[o, slot], self.s_send.at[t], self.s_recv.at[o, slot],
                      self.place.along(b, g))

    def third_copy(self, o, d):
        b = (o + 2) % 3
        p = self.place.xyz[b]
        return remote(self.t_buf.at[o, p], self.t_buf.at[o, p], self.t_sem.at[o, d - 1, 0], self.t_sem.at[o, d - 1, 1],
                      self.place.along(b, (p + d) % 4))

    def third_wait(self, o, d):
        p = (self.place.xyz[(o + 2) % 3] + 4 - d) % 4
        return remote(self.t_buf.at[o, p], self.t_buf.at[o, p], self.t_sem.at[o, d - 1, 0], self.t_sem.at[o, d - 1, 1],
                      self.place.other())

    def rows(self, t, q):
        return self.out.at[t, pl.ds(self.place.core * HALF + q * QUART, QUART)]

    def gather2_copy(self, t, o, d):
        b = (o + 1) % 3
        ref = self.rows(t, self.place.xyz[o])
        return remote(ref, ref, self.g2_send.at[o, d - 1], self.g2_recv.at[t],
                      self.place.along(b, (self.place.xyz[b] + d) % 4))

    def gather1_copy(self, t, o, d):
        p = self.place.xyz[o]
        ref = self.rows(t, p)
        return remote(ref, ref, self.g1_sem.at[t, d - 1, 0], self.g1_sem.at[t, d - 1, 1],
                      self.place.along(o, (p + d) % 4))

    def gather1_wait(self, t, o, d):
        ref = self.rows(t, (self.place.xyz[o] + 4 - d) % 4)
        return remote(ref, ref, self.g1_sem.at[t, d - 1, 0], self.g1_sem.at[t, d - 1, 1], self.place.other())

    def gatherc_copy(self, t):
        ref = self.out.at[t, pl.ds(self.place.core * HALF, HALF)]
        return remote(ref, ref, self.gc_sem.at[t, 0], self.gc_sem.at[t, 1], self.place.other())

    def gatherc_wait(self, t):
        ref = self.out.at[t, pl.ds((1 - self.place.core) * HALF, HALF)]
        return remote(ref, ref, self.gc_sem.at[t, 0], self.gc_sem.at[t, 1], self.place.other())

    def step0(self, g):
        for o in range(3):
            t = 3 * g + o
            self.c_out[t] = self.part[t, pl.ds((1 - self.place.core) * HALF, HALF)].astype(BF)
            self.core_copy(t).start()

    def step1(self, g):
        for o in range(3):
            t = 3 * g + o
            self.core_copy(t).wait_recv()
            mine = pl.ds(self.place.core * HALF, HALF)
            total = self.part[t, mine] + self.c_in[t].astype(F32)
            self.part[t, mine] = total
            self.q_out[t] = total.astype(BF)
            for d in (2, 1, 3):
                self.quarter_copy(t, o, d).start()

    def step2(self, g):
        for o in range(3):
            t = 3 * g + o
            row = self.place.core * HALF + self.place.xyz[o] * QUART
            total = self.part[t, pl.ds(row, QUART)]
            for d in (1, 3, 2):
                self.quarter_copy(t, o, d).wait_recv()
                total = total + self.q_in[t, d - 1].astype(F32)
            self.q_own[t] = total
            self.s_out[t] = total.astype(BF)
            p = self.place.xyz[(o + 1) % 3]

            @pl.when(p != g)
            def _():
                self.second_copy(t, o, g, (p + 4 - g) % 4 - 1).start()

    def step3(self, g):
        for o in range(3):
            t = 3 * g + o
            p = self.place.xyz[(o + 1) % 3]

            @pl.when(p == g)
            def _():
                total = self.q_own[t]
                for slot in range(3):
                    self.second_copy(t, o, g, slot).wait_recv()
                    total = total + self.s_in[o, slot].astype(F32)
                self.t_buf[o, self.place.xyz[(o + 2) % 3]] = total.astype(BF)
                for d in (2, 1, 3):
                    self.third_copy(o, d).start()

    def step4(self, g):
        for o in range(3):
            t = 3 * g + o
            p = self.place.xyz[(o + 1) % 3]

            @pl.when(p == g)
            def _():
                for d in (1, 3, 2):
                    self.third_wait(o, d).wait_recv()
                buf = self.t_buf
                total = (buf[o, 0].astype(F32) + buf[o, 1].astype(F32)) + (buf[o, 2].astype(F32) + buf[o, 3].astype(F32))
                row = self.place.core * HALF + self.place.xyz[o] * QUART
                self.out[t, pl.ds(row, QUART)] = total.astype(BF)
                for d in (2, 1, 3):
                    self.gather2_copy(t, o, d).start()

    def step5(self, g):
        for o in range(3):
            t = 3 * g + o
            p = self.place.xyz[(o + 1) % 3]

            @pl.when(p != g)
            def _():
                self.gather2_copy(t, o, 1).wait_recv()

            for d in (2, 1, 3):
                self.gather1_copy(t, o, d).start()

    def step6(self, g):
        for o in range(3):
            t = 3 * g + o
            for d in (1, 3, 2):
                self.gather1_wait(t, o, d).wait_recv()
            self.gatherc_copy(t).start()

    def step7(self, g):
        for o in range(3):
            self.gatherc_wait(3 * g + o).wait_recv()

    def sends(self, g):
        for o in range(3):
            t = 3 * g + o
            p = self.place.xyz[(o + 1) % 3]
            self.core_copy(t).wait_send()
            for d in (1, 2, 3):
                self.quarter_copy(t, o, d).wait_send()
                self.gather1_copy(t, o, d).wait_send()
            self.gatherc_copy(t).wait_send()

            @pl.when(p != g)
            def _():
                self.second_copy(t, o, g, (p + 4 - g) % 4 - 1).wait_send()

            @pl.when(p == g)
            def _():
                for d in (1, 2, 3):
                    self.third_copy(o, d).wait_send()
                    self.gather2_copy(t, o, d).wait_send()


def greet(place, halos):
    barrier = pltpu.get_barrier_semaphore()
    friends = [place.other()]
    for axis in range(3):
        for d in (1, 2, 3):
            friends.append(place.along(axis, (place.xyz[axis] + d) % 4))
    if halos:
        friends.append(((place.tm + 1) % 4, place.height))
        friends.append(((place.tm + 3) % 4, place.height))
        friends.append((place.tm, (place.height + 1) % 32))
        friends.append((place.tm, (place.height + 31) % 32))
    for device in friends:
        pl.semaphore_signal(barrier, inc=1, device_id=device, device_id_type=MESH)
    pl.semaphore_wait(barrier, len(friends))


def reduce_kernel(part_ref, out_ref, part, *refs):
    place = Place()
    greet(place, False)
    part[...] = part_ref[...]
    red = Reduce(place, part, out_ref, refs)
    steps = [red.step0, red.step1, red.step2, red.step3, red.step4, red.step5, red.step6, red.step7, red.sends]
    for step in steps:
        @pl.loop(0, 4)
        def _(g):
            step(g)


def reduced(partial):
    return pl.pallas_call(
        reduce_kernel,
        out_shape=jax.ShapeDtypeStruct((12, 384, 384), BF),
        in_specs=[pl.BlockSpec(memory_space=pltpu.VMEM)],
        out_specs=pl.BlockSpec(memory_space=pltpu.VMEM),
        scratch_shapes=[pltpu.VMEM((12, 384, 384), F32)] + Reduce.SCRATCH,
        compiler_params=pltpu.CompilerParams(
            collective_id=0, has_side_effects=True, vmem_limit_bytes=56 * 2**20),
    )(partial)


def shifted(array, axis, by):
    size = lax.axis_size(axis)
    pairs = [(i, i + by) for i in range(size) if 0 <= i + by < size]
    return lax.ppermute(array, axis, pairs)


def extended(array, sides, width):
    for axis, dim in sides:
        size, length = (lax.axis_size(axis), array.shape[dim])
        up = [(i, (i + 1) % size) for i in range(size - 1)]
        down = [(j, i) for i, j in up]
        last = lax.slice_in_dim(array, length - width, length, axis=dim)
        first = lax.slice_in_dim(array, 0, width, axis=dim)
        before = lax.ppermute(last, axis, up)
        after = lax.ppermute(first, axis, down)
        array = jnp.concatenate([before, array, after], axis=dim)
    return array


def flat(value):
    return value.reshape(-1, value.shape[-1])


def inner(left, right):
    return lax.dot_general(
        left, right, (((0,), (0,)), ((), ())), preferred_element_type=jnp.float32
    )


def backward(left, weight):
    return lax.dot_general(
        left, weight, (((1,), (1,)), ((), ())), preferred_element_type=jnp.float32
    )


def on_device(latents, cotangent, temporal_weight, spatial_weight):
    frames, rows, cols, chans = latents.shape
    count = frames * lax.axis_size("tm") * rows * lax.axis_size("height") * cols
    scale = 1.0 / math.sqrt(count)
    earlier = shifted(latents, "tm", 1)
    before = jnp.concatenate([earlier, latents], axis=0)
    pre = jnp.zeros((frames * rows * cols, chans), jnp.float32)
    for tap in range(3):
        pre = pre + jnp.dot(
            flat(before[2 - tap : 2 - tap + frames]),
            temporal_weight[tap],
            preferred_element_type=jnp.float32,
        )
    hidden = jax.nn.silu(pre).astype(jnp.bfloat16)
    rimmed = extended(cotangent, (("height", 1),), 1)
    padded = jnp.pad(rimmed, ((0, 0), (0, 0), (1, 1), (0, 0)))
    back = jnp.zeros((frames * rows * cols, chans), jnp.float32)
    spatial = []
    for i in range(3):
        for j in range(3):
            window = flat(padded[:, 2 - i : 2 - i + rows, 2 - j : 2 - j + cols])
            back = back + backward(window, spatial_weight[i, j])
            spatial.append(inner(hidden, window))
    sigma = jax.nn.sigmoid(pre)
    pre_grad = (back * sigma * (1.0 + pre * (1.0 - sigma))).astype(jnp.bfloat16)
    grid = pre_grad.reshape(frames, rows, cols, chans)
    temporal = []
    for tap in range(3):
        temporal.append(inner(flat(before[2 - tap : 2 - tap + frames]), pre_grad))
    total = flat(cotangent).astype(jnp.float32)
    later = shifted(grid, "tm", -1)
    after = jnp.concatenate([grid, later], axis=0)
    for tap in range(3):
        total = total + backward(flat(after[tap : tap + frames]), temporal_weight[tap])
    latent_grad = total.reshape(frames, rows, cols, chans).astype(jnp.bfloat16)
    total = reduced(jnp.stack(spatial + temporal)).astype(jnp.float32) * scale
    return (latent_grad, total[9:], total[:9].reshape(3, 3, chans, chans))


def solution(mesh):
    return jax.shard_map(
        on_device,
        mesh=mesh,
        in_specs=(P("tm", "height", None, None), P("tm", "height", None, None), P(), P()),
        out_specs=(P("tm", "height", None, None), P(), P()),
        check_vma=False,
    )
```

```python
import math

import jax
import jax.numpy as jnp
from jax import lax
from jax.experimental import pallas as pl
from jax.experimental.pallas import tpu as pltpu
from jax.sharding import PartitionSpec as P

BF = jnp.bfloat16
F32 = jnp.float32
MESH = pl.DeviceIdType.MESH
HALF = 192
QUART = 48


class Place:
    def __init__(self):
        tm = lax.axis_index("tm")
        height = lax.axis_index("height")
        self.tm = tm
        self.height = height
        self.core = tm % 2
        self.xyz = (height % 4, (height // 16) * 2 + tm // 2, (height // 4) % 4)

    def at(self, x, y, z, core):
        return ((y % 2) * 2 + core, (y // 2) * 16 + z * 4 + x)

    def along(self, axis, where):
        xyz = list(self.xyz)
        xyz[axis] = where
        return self.at(*xyz, self.core)

    def other(self):
        return (self.tm + 1 - 2 * self.core, self.height)


def remote(src, dst, send, recv, device):
    return pltpu.make_async_remote_copy(
        src_ref=src, dst_ref=dst, send_sem=send, recv_sem=recv,
        device_id=device, device_id_type=MESH)


class Reduce:
    SCRATCH = [
        pltpu.VMEM((12, HALF, 384), BF),
        pltpu.VMEM((12, HALF, 384), BF),
        pltpu.VMEM((12, HALF, 384), BF),
        pltpu.VMEM((12, QUART, 384), F32),
        pltpu.VMEM((12, 3, QUART, 384), BF),
        pltpu.VMEM((12, QUART, 384), BF),
        pltpu.VMEM((3, 3, QUART, 384), BF),
        pltpu.VMEM((3, 4, QUART, 384), BF),
        pltpu.SemaphoreType.DMA((12, 2)),
        pltpu.SemaphoreType.DMA((12, 3, 2)),
        pltpu.SemaphoreType.DMA((12,)),
        pltpu.SemaphoreType.DMA((3, 3)),
        pltpu.SemaphoreType.DMA((3, 3, 2)),
        pltpu.SemaphoreType.DMA((3, 3)),
        pltpu.SemaphoreType.DMA((12,)),
        pltpu.SemaphoreType.DMA((12, 3, 2)),
        pltpu.SemaphoreType.DMA((12, 2)),
    ]

    def __init__(self, place, part, out, refs):
        self.place = place
        self.part = part
        self.out = out
        (self.c_out, self.c_in, self.q_out, self.q_own, self.q_in, self.s_out, self.s_in, self.t_buf,
         self.c_sem, self.q_sem, self.s_send, self.s_recv, self.t_sem, self.g2_send, self.g2_recv,
         self.g1_sem, self.gc_sem) = refs

    def core_copy(self, t):
        return remote(self.c_out.at[t], self.c_in.at[t], self.c_sem.at[t, 0], self.c_sem.at[t, 1], self.place.other())

    def quarter_copy(self, t, o, d):
        q = (self.place.xyz[o] + d) % 4
        return remote(self.q_out.at[t, pl.ds(q * QUART, QUART)], self.q_in.at[t, d - 1],
                      self.q_sem.at[t, d - 1, 0], self.q_sem.at[t, d - 1, 1], self.place.along(o, q))

    def second_copy(self, t, o, g, slot):
        b = (o + 1) % 3
        return remote(self.s_out.at[t], self.s_in.at[o, slot], self.s_send.at[t], self.s_recv.at[o, slot],
                      self.place.along(b, g))

    def third_copy(self, o, d):
        b = (o + 2) % 3
        p = self.place.xyz[b]
        return remote(self.t_buf.at[o, p], self.t_buf.at[o, p], self.t_sem.at[o, d - 1, 0], self.t_sem.at[o, d - 1, 1],
                      self.place.along(b, (p + d) % 4))

    def third_wait(self, o, d):
        p = (self.place.xyz[(o + 2) % 3] + 4 - d) % 4
        return remote(self.t_buf.at[o, p], self.t_buf.at[o, p], self.t_sem.at[o, d - 1, 0], self.t_sem.at[o, d - 1, 1],
                      self.place.other())

    def rows(self, t, q):
        return self.out.at[t, pl.ds(self.place.core * HALF + q * QUART, QUART)]

    def gather2_copy(self, t, o, d):
        b = (o + 1) % 3
        ref = self.rows(t, self.place.xyz[o])
        return remote(ref, ref, self.g2_send.at[o, d - 1], self.g2_recv.at[t],
                      self.place.along(b, (self.place.xyz[b] + d) % 4))

    def gather1_copy(self, t, o, d):
        p = self.place.xyz[o]
        ref = self.rows(t, p)
        return remote(ref, ref, self.g1_sem.at[t, d - 1, 0], self.g1_sem.at[t, d - 1, 1],
                      self.place.along(o, (p + d) % 4))

    def gather1_wait(self, t, o, d):
        ref = self.rows(t, (self.place.xyz[o] + 4 - d) % 4)
        return remote(ref, ref, self.g1_sem.at[t, d - 1, 0], self.g1_sem.at[t, d - 1, 1], self.place.other())

    def gatherc_copy(self, t):
        ref = self.out.at[t, pl.ds(self.place.core * HALF, HALF)]
        return remote(ref, ref, self.gc_sem.at[t, 0], self.gc_sem.at[t, 1], self.place.other())

    def gatherc_wait(self, t):
        ref = self.out.at[t, pl.ds((1 - self.place.core) * HALF, HALF)]
        return remote(ref, ref, self.gc_sem.at[t, 0], self.gc_sem.at[t, 1], self.place.other())

    def step0(self, g):
        for o in range(3):
            t = 3 * g + o
            self.c_out[t] = self.part[g, pl.ds((1 - self.place.core) * HALF, HALF), o * 384:(o + 1) * 384].astype(BF)
            self.core_copy(t).start()

    def step1(self, g):
        for o in range(3):
            t = 3 * g + o
            self.core_copy(t).wait_recv()
            mine = (g, pl.ds(self.place.core * HALF, HALF), slice(o * 384, (o + 1) * 384))
            total = self.part[mine] + self.c_in[t].astype(F32)
            self.part[mine] = total
            self.q_out[t] = total.astype(BF)
            for d in (2, 1, 3):
                self.quarter_copy(t, o, d).start()

    def step2(self, g):
        for o in range(3):
            t = 3 * g + o
            row = self.place.core * HALF + self.place.xyz[o] * QUART
            total = self.part[g, pl.ds(row, QUART), o * 384:(o + 1) * 384]
            for d in (1, 3, 2):
                self.quarter_copy(t, o, d).wait_recv()
                total = total + self.q_in[t, d - 1].astype(F32)
            self.q_own[t] = total
            self.s_out[t] = total.astype(BF)
            p = self.place.xyz[(o + 1) % 3]

            @pl.when(p != g)
            def _():
                self.second_copy(t, o, g, (p + 4 - g) % 4 - 1).start()

    def step3(self, g):
        for o in range(3):
            t = 3 * g + o
            p = self.place.xyz[(o + 1) % 3]

            @pl.when(p == g)
            def _():
                total = self.q_own[t]
                for slot in range(3):
                    self.second_copy(t, o, g, slot).wait_recv()
                    total = total + self.s_in[o, slot].astype(F32)
                self.t_buf[o, self.place.xyz[(o + 2) % 3]] = total.astype(BF)
                for d in (2, 1, 3):
                    self.third_copy(o, d).start()

    def step4(self, g):
        for o in range(3):
            t = 3 * g + o
            p = self.place.xyz[(o + 1) % 3]

            @pl.when(p == g)
            def _():
                for d in (1, 3, 2):
                    self.third_wait(o, d).wait_recv()
                buf = self.t_buf
                total = (buf[o, 0].astype(F32) + buf[o, 1].astype(F32)) + (buf[o, 2].astype(F32) + buf[o, 3].astype(F32))
                row = self.place.core * HALF + self.place.xyz[o] * QUART
                self.out[t, pl.ds(row, QUART)] = total.astype(BF)
                for d in (2, 1, 3):
                    self.gather2_copy(t, o, d).start()

    def step5(self, g):
        for o in range(3):
            t = 3 * g + o
            p = self.place.xyz[(o + 1) % 3]

            @pl.when(p != g)
            def _():
                self.gather2_copy(t, o, 1).wait_recv()

            for d in (2, 1, 3):
                self.gather1_copy(t, o, d).start()

    def step6(self, g):
        for o in range(3):
            t = 3 * g + o
            for d in (1, 3, 2):
                self.gather1_wait(t, o, d).wait_recv()
            self.gatherc_copy(t).start()

    def step7(self, g):
        for o in range(3):
            self.gatherc_wait(3 * g + o).wait_recv()

    def sends(self, g):
        for o in range(3):
            t = 3 * g + o
            p = self.place.xyz[(o + 1) % 3]
            self.core_copy(t).wait_send()
            for d in (1, 2, 3):
                self.quarter_copy(t, o, d).wait_send()
                self.gather1_copy(t, o, d).wait_send()
            self.gatherc_copy(t).wait_send()

            @pl.when(p != g)
            def _():
                self.second_copy(t, o, g, (p + 4 - g) % 4 - 1).wait_send()

            @pl.when(p == g)
            def _():
                for d in (1, 2, 3):
                    self.third_copy(o, d).wait_send()
                    self.gather2_copy(t, o, d).wait_send()


def greet(place, halos):
    barrier = pltpu.get_barrier_semaphore()
    friends = [place.other()]
    for axis in range(3):
        for d in (1, 2, 3):
            friends.append(place.along(axis, (place.xyz[axis] + d) % 4))
    if halos:
        friends.append(((place.tm + 1) % 4, place.height))
        friends.append(((place.tm + 3) % 4, place.height))
        friends.append((place.tm, (place.height + 1) % 32))
        friends.append((place.tm, (place.height + 31) % 32))
    for device in friends:
        pl.semaphore_signal(barrier, inc=1, device_id=device, device_id_type=MESH)
    pl.semaphore_wait(barrier, len(friends))


BOUNDS = (0, 144, 272, 400, 528, 640)
CHUNKS = 5
CW = 128


def nt(left, right):
    return lax.dot_general(left, right, (((1,), (1,)), ((), ())), preferred_element_type=F32)


def tn(left, right):
    return lax.dot_general(left, right, (((0,), (0,)), ((), ())), preferred_element_type=F32)


def lanes(*values):
    return jnp.concatenate(values, axis=1)


def shifts(cot3, row, f, start, size):
    low, high = max(start - 16, 0), min(start + size + 16, 640)
    n = high - low
    for b in range(3):
        x = cot3[row, f, low:high, 384 + b * 128:384 + (b + 1) * 128].astype(F32)
        place = lax.broadcasted_iota(jnp.int32, (n, 128), 0)
        after = pltpu.roll(x, n - 1, 0)
        before = pltpu.roll(x, 1, 0)
        if high == 640:
            after = jnp.where(place == n - 1, 0.0, after)
        if low == 0:
            before = jnp.where(place == 0, 0.0, before)
        at = start - low
        cot3[row, f, start:start + size, b * 128:(b + 1) * 128] = after[at:at + size].astype(BF)
        cot3[row, f, start:start + size, 768 + b * 128:768 + (b + 1) * 128] = before[at:at + size].astype(BF)


def block_kernel(lat_hbm, cot_hbm, tw_hbm, sw_hbm, lg_hbm, tg_hbm, sg_hbm,
                 lat, cot3, back, hid, pgx, tw, twt, sw, part, out, lg,
                 in_sem, w_sem, l_sem, u_sem, d_sem, p_sem, o_sem, *refs):
    place = Place()
    tm, height = place.tm, place.height
    cot_in = [pltpu.make_async_copy(cot_hbm.at[:, r], cot3.at[r + 1, :, :, 384:768], in_sem.at[r]) for r in range(2)]
    lat_in = pltpu.make_async_copy(lat_hbm, lat.at[2:4], in_sem.at[2])
    tw_in = pltpu.make_async_copy(tw_hbm, tw, in_sem.at[3])
    sw_in = [pltpu.make_async_copy(sw_hbm.at[i, j], sw.at[i, :, j * 384:(j + 1) * 384], w_sem.at[3 * i + j])
             for i in (1, 0, 2) for j in range(3)]
    twt_in = [pltpu.make_async_copy(tw_hbm.at[k], twt.at[:, k * 384:(k + 1) * 384], w_sem.at[9 + k]) for k in range(3)]
    for copy in cot_in + sw_in + [lat_in, tw_in] + twt_in:
        copy.start()

    greet(place, True)

    def l_copy(c):
        cols = pl.ds(c * CW, CW)
        return remote(lat_hbm.at[:, :, cols], lat.at[0:2, :, cols], l_sem.at[c, 0], l_sem.at[c, 1],
                      ((tm + 1) % 4, height))

    def down_copy(c):
        cols = pl.ds(BOUNDS[c], BOUNDS[c + 1] - BOUNDS[c])
        return remote(cot_hbm.at[:, 1, cols], cot3.at[0, :, cols, 384:768], d_sem.at[c, 0], d_sem.at[c, 1],
                      (tm, (height + 1) % 32))

    def up_copy(c):
        cols = pl.ds(BOUNDS[c], BOUNDS[c + 1] - BOUNDS[c])
        return remote(cot_hbm.at[:, 0, cols], cot3.at[3, :, cols, 384:768], u_sem.at[c, 0], u_sem.at[c, 1],
                      (tm, (height + 31) % 32))

    def p_copy(c):
        cols = pl.ds(c * CW, CW)
        return remote(pgx.at[0:2, :, cols], pgx.at[2:4, :, cols], p_sem.at[c, 0], p_sem.at[c, 1],
                      ((tm + 3) % 4, height))

    for c in range(CHUNKS):
        @pl.when(tm < 3)
        def _():
            l_copy(c).start()

        @pl.when(height < 31)
        def _():
            down_copy(c).start()

        @pl.when(height > 0)
        def _():
            up_copy(c).start()

    @pl.when(tm == 0)
    def _():
        lat[0:2] = jnp.zeros((2, 2, 640, 384), BF)

    @pl.when(tm == 3)
    def _():
        pgx[2:4] = jnp.zeros((2, 2, 640, 384), BF)

    @pl.when(height == 0)
    def _():
        cot3[0, :, :, 384:768] = jnp.zeros((2, 640, 384), BF)

    @pl.when(height == 31)
    def _():
        cot3[3, :, :, 384:768] = jnp.zeros((2, 640, 384), BF)

    for copy in cot_in:
        copy.wait()
    for row in (1, 2):
        for f in range(2):
            shifts(cot3, row, f, 0, 640)
    for copy in sw_in:
        copy.wait()
    for f in range(2):
        back[0, f] = nt(lanes(cot3[1, f], cot3[2, f]), lanes(sw[1], sw[0]))
        back[1, f] = nt(lanes(cot3[2, f], cot3[1, f]), lanes(sw[1], sw[2]))
    lat_in.wait()
    tw_in.wait()
    for copy in twt_in:
        copy.wait()

    weight = tw.reshape(1152, 384)
    for c in range(CHUNKS):
        cols = slice(c * CW, (c + 1) * CW)

        @pl.when(tm > 0)
        def _():
            l_copy(c).wait_recv()

        @pl.when(height > 0)
        def _():
            down_copy(c).wait_recv()

        @pl.when(height < 31)
        def _():
            up_copy(c).wait_recv()

        for row in (0, 3):
            for f in range(2):
                shifts(cot3, row, f, c * CW, CW)
        for r in range(2):
            halo, i = (0, 2) if r == 0 else (3, 0)
            window = jnp.concatenate([cot3[halo, f, cols] for f in range(2)], axis=0)
            total = nt(window, sw[i]) + jnp.concatenate([back[r, f, cols] for f in range(2)], axis=0)
            left = jnp.concatenate(
                [lanes(lat[f + 2, r, cols], lat[f + 1, r, cols], lat[f, r, cols]) for f in range(2)], axis=0)
            pre = jnp.dot(left, weight[...], preferred_element_type=F32)
            sigma = jax.nn.sigmoid(pre)
            hidden = (pre * sigma).astype(BF)
            grad = (total * sigma * (1.0 + pre * (1.0 - sigma))).astype(BF)
            for f in range(2):
                hid[r, f, cols] = hidden[f * CW:(f + 1) * CW]
                pgx[f, r, cols] = grad[f * CW:(f + 1) * CW]

        @pl.when(tm > 0)
        def _():
            p_copy(c).start()

    red = Reduce(place, part, out, refs)

    def spatial(i, r):
        value = tn(hid[r].reshape(1280, 384), cot3[r + 2 - i].reshape(1280, 1152))
        part[i] = value if r == 0 else part[i] + value

    def temporal(f):
        grads = lanes(*(pgx[f + k].reshape(1280, 384) for k in range(3)))
        value = tn(lat[f + 2].reshape(1280, 384), grads)
        part[3] = value if f == 0 else part[3] + value

    def latent(f, r):
        grads = lanes(*(pgx[f + k, r] for k in range(3)))
        lg[f, r] = (cot3[r + 1, f, :, 384:768].astype(F32) + nt(grads, twt[...])).astype(BF)
        pltpu.make_async_copy(lg.at[f, r], lg_hbm.at[f, r], o_sem.at[4 + 2 * f + r]).start()

    def store(g):
        target = sg_hbm.at[g] if g < 3 else tg_hbm
        return pltpu.make_async_copy(out.at[3 * g:3 * g + 3], target, o_sem.at[g])

    def arrive():
        for c in range(CHUNKS):
            @pl.when(tm < 3)
            def _():
                p_copy(c).wait_recv()

    def last(g):
        red.step7(g)
        store(g).start()

    spatial(0, 0)
    spatial(0, 1)
    red.step0(0)
    spatial(1, 0)
    red.step1(0)
    spatial(1, 1)
    red.step0(1)
    red.step2(0)
    spatial(2, 0)
    red.step1(1)
    red.step3(0)
    spatial(2, 1)
    red.step0(2)
    red.step2(1)
    red.step4(0)
    arrive()
    temporal(0)
    red.step1(2)
    red.step3(1)
    red.step5(0)
    temporal(1)
    red.step0(3)
    red.step2(2)
    red.step4(1)
    red.step6(0)
    latent(0, 0)
    red.step1(3)
    red.step3(2)
    red.step5(1)
    last(0)
    latent(0, 1)
    red.step2(3)
    red.step4(2)
    red.step6(1)
    latent(1, 0)
    red.step3(3)
    red.step5(2)
    last(1)
    latent(1, 1)
    red.step4(3)
    red.step6(2)
    red.step5(3)
    last(2)
    red.step6(3)
    last(3)

    for c in range(CHUNKS):
        @pl.when(tm < 3)
        def _():
            l_copy(c).wait_send()

        @pl.when(height < 31)
        def _():
            down_copy(c).wait_send()

        @pl.when(height > 0)
        def _():
            up_copy(c).wait_send()

        @pl.when(tm > 0)
        def _():
            p_copy(c).wait_send()
    for g in range(4):
        red.sends(g)
        store(g).wait()
    for f in range(2):
        for r in range(2):
            pltpu.make_async_copy(lg.at[f, r], lg_hbm.at[f, r], o_sem.at[4 + 2 * f + r]).wait()


def on_device(latents, cotangent, temporal_weight, spatial_weight):
    frames, rows, cols, chans = latents.shape
    count = frames * lax.axis_size("tm") * rows * lax.axis_size("height") * cols
    scale = 1.0 / math.sqrt(count)
    anywhere = pl.BlockSpec(memory_space=pl.ANY)
    latent_grad, temporal, spatial = pl.pallas_call(
        block_kernel,
        out_shape=(
            jax.ShapeDtypeStruct((2, 2, 640, 384), BF),
            jax.ShapeDtypeStruct((3, 384, 384), BF),
            jax.ShapeDtypeStruct((3, 3, 384, 384), BF),
        ),
        in_specs=[anywhere] * 4,
        out_specs=(anywhere,) * 3,
        scratch_shapes=[
            pltpu.VMEM((4, 2, 640, 384), BF),
            pltpu.VMEM((4, 2, 640, 1152), BF),
            pltpu.VMEM((2, 2, 640, 384), F32),
            pltpu.VMEM((2, 2, 640, 384), BF),
            pltpu.VMEM((4, 2, 640, 384), BF),
            pltpu.VMEM((3, 384, 384), BF),
            pltpu.VMEM((384, 1152), BF),
            pltpu.VMEM((3, 384, 1152), BF),
            pltpu.VMEM((4, 384, 1152), F32),
            pltpu.VMEM((12, 384, 384), BF),
            pltpu.VMEM((2, 2, 640, 384), BF),
            pltpu.SemaphoreType.DMA((4,)),
            pltpu.SemaphoreType.DMA((12,)),
            pltpu.SemaphoreType.DMA((CHUNKS, 2)),
            pltpu.SemaphoreType.DMA((CHUNKS, 2)),
            pltpu.SemaphoreType.DMA((CHUNKS, 2)),
            pltpu.SemaphoreType.DMA((CHUNKS, 2)),
            pltpu.SemaphoreType.DMA((8,)),
        ] + Reduce.SCRATCH,
        compiler_params=pltpu.CompilerParams(
            collective_id=0, has_side_effects=True, vmem_limit_bytes=60 * 2**20),
    )(latents, cotangent, temporal_weight, spatial_weight)
    return (latent_grad, temporal.astype(F32) * scale, spatial.astype(F32) * scale)


def solution(mesh):
    return jax.shard_map(
        on_device,
        mesh=mesh,
        in_specs=(P("tm", "height", None, None), P("tm", "height", None, None), P(), P()),
        out_specs=(P("tm", "height", None, None), P(), P()),
        check_vma=False,
    )
```

```python
import functools
import math

import jax
import jax.numpy as jnp
from jax import lax
from jax.experimental import pallas as pl
from jax.experimental.pallas import tpu as pltpu
from jax.sharding import PartitionSpec as P

BF = jnp.bfloat16
F32 = jnp.float32
MESH = pl.DeviceIdType.MESH
HALF = 192
QUART = 48


class Place:
    def __init__(self):
        tm = lax.axis_index("tm")
        height = lax.axis_index("height")
        self.tm = tm
        self.height = height
        self.core = tm % 2
        self.xyz = (height % 4, (height // 16) * 2 + tm // 2, (height // 4) % 4)
        x, y, z = self.xyz
        self.corner = ((x == 0) | (x == 3)) & ((z == 0) | (z == 3))
        self.diagonal = self.corner & (x == z)
        self.half = height // 16
        self.mirror = self.at(x, (y + 2) % 4, z, self.core)
        self.opposite = self.at(3 - x, y, 3 - z, self.core)

    def at(self, x, y, z, core):
        return ((y % 2) * 2 + core, (y // 2) * 16 + z * 4 + x)

    def along(self, axis, where):
        xyz = list(self.xyz)
        xyz[axis] = where
        return self.at(*xyz, self.core)

    def other(self):
        return (self.tm + 1 - 2 * self.core, self.height)


def remote(src, dst, send, recv, device):
    return pltpu.make_async_remote_copy(
        src_ref=src, dst_ref=dst, send_sem=send, recv_sem=recv,
        device_id=device, device_id_type=MESH)


class Reduce:
    SCRATCH = [
        pltpu.VMEM((12, HALF, 384), BF),
        pltpu.VMEM((12, HALF, 384), BF),
        pltpu.VMEM((12, HALF, 384), BF),
        pltpu.VMEM((12, QUART, 384), F32),
        pltpu.VMEM((12, 3, QUART, 384), BF),
        pltpu.VMEM((12, QUART, 384), BF),
        pltpu.VMEM((3, 3, QUART, 384), BF),
        pltpu.VMEM((3, 4, QUART, 384), BF),
        pltpu.SemaphoreType.DMA((12, 2)),
        pltpu.SemaphoreType.DMA((12, 3, 2)),
        pltpu.SemaphoreType.DMA((12,)),
        pltpu.SemaphoreType.DMA((3, 3)),
        pltpu.SemaphoreType.DMA((3, 3, 2)),
        pltpu.SemaphoreType.DMA((3, 3)),
        pltpu.SemaphoreType.DMA((12,)),
        pltpu.SemaphoreType.DMA((12, 3, 2)),
        pltpu.SemaphoreType.DMA((12, 2)),
    ]

    def __init__(self, place, part, out, refs):
        self.place = place
        self.part = part
        self.out = out
        (self.c_out, self.c_in, self.q_out, self.q_own, self.q_in, self.s_out, self.s_in, self.t_buf,
         self.c_sem, self.q_sem, self.s_send, self.s_recv, self.t_sem, self.g2_send, self.g2_recv,
         self.g1_sem, self.gc_sem) = refs

    def core_copy(self, t):
        return remote(self.c_out.at[t], self.c_in.at[t], self.c_sem.at[t, 0], self.c_sem.at[t, 1], self.place.other())

    def quarter_copy(self, t, o, d):
        q = (self.place.xyz[o] + d) % 4
        return remote(self.q_out.at[t, pl.ds(q * QUART, QUART)], self.q_in.at[t, d - 1],
                      self.q_sem.at[t, d - 1, 0], self.q_sem.at[t, d - 1, 1], self.place.along(o, q))

    def second_copy(self, t, o, g, slot):
        b = (o + 1) % 3
        return remote(self.s_out.at[t], self.s_in.at[o, slot], self.s_send.at[t], self.s_recv.at[o, slot],
                      self.place.along(b, g))

    def third_copy(self, o, d):
        b = (o + 2) % 3
        p = self.place.xyz[b]
        return remote(self.t_buf.at[o, p], self.t_buf.at[o, p], self.t_sem.at[o, d - 1, 0], self.t_sem.at[o, d - 1, 1],
                      self.place.along(b, (p + d) % 4))

    def third_wait(self, o, d):
        p = (self.place.xyz[(o + 2) % 3] + 4 - d) % 4
        return remote(self.t_buf.at[o, p], self.t_buf.at[o, p], self.t_sem.at[o, d - 1, 0], self.t_sem.at[o, d - 1, 1],
                      self.place.other())

    def rows(self, t, q):
        return self.out.at[t, pl.ds(self.place.core * HALF + q * QUART, QUART)]

    def gather2_copy(self, t, o, d):
        b = (o + 1) % 3
        ref = self.rows(t, self.place.xyz[o])
        return remote(ref, ref, self.g2_send.at[o, d - 1], self.g2_recv.at[t],
                      self.place.along(b, (self.place.xyz[b] + d) % 4))

    def gather1_copy(self, t, o, d):
        p = self.place.xyz[o]
        ref = self.rows(t, p)
        return remote(ref, ref, self.g1_sem.at[t, d - 1, 0], self.g1_sem.at[t, d - 1, 1],
                      self.place.along(o, (p + d) % 4))

    def gather1_wait(self, t, o, d):
        ref = self.rows(t, (self.place.xyz[o] + 4 - d) % 4)
        return remote(ref, ref, self.g1_sem.at[t, d - 1, 0], self.g1_sem.at[t, d - 1, 1], self.place.other())

    def gatherc_copy(self, t):
        ref = self.out.at[t, pl.ds(self.place.core * HALF, HALF)]
        return remote(ref, ref, self.gc_sem.at[t, 0], self.gc_sem.at[t, 1], self.place.other())

    def gatherc_wait(self, t):
        ref = self.out.at[t, pl.ds((1 - self.place.core) * HALF, HALF)]
        return remote(ref, ref, self.gc_sem.at[t, 0], self.gc_sem.at[t, 1], self.place.other())

    def step0(self, g):
        for o in range(3):
            t = 3 * g + o
            self.c_out[t] = self.part[g, pl.ds((1 - self.place.core) * HALF, HALF), o * 384:(o + 1) * 384].astype(BF)
            self.core_copy(t).start()

    def step1(self, g):
        for o in range(3):
            t = 3 * g + o
            self.core_copy(t).wait_recv()
            mine = (g, pl.ds(self.place.core * HALF, HALF), slice(o * 384, (o + 1) * 384))
            total = self.part[mine] + self.c_in[t].astype(F32)
            self.part[mine] = total
            self.q_out[t] = total.astype(BF)
            for d in (2, 1, 3):
                self.quarter_copy(t, o, d).start()

    def step2(self, g):
        for o in range(3):
            t = 3 * g + o
            row = self.place.core * HALF + self.place.xyz[o] * QUART
            total = self.part[g, pl.ds(row, QUART), o * 384:(o + 1) * 384]
            for d in (1, 3, 2):
                self.quarter_copy(t, o, d).wait_recv()
                total = total + self.q_in[t, d - 1].astype(F32)
            self.q_own[t] = total
            self.s_out[t] = total.astype(BF)
            p = self.place.xyz[(o + 1) % 3]

            @pl.when(p != g)
            def _():
                self.second_copy(t, o, g, (p + 4 - g) % 4 - 1).start()

    def step3(self, g):
        for o in range(3):
            t = 3 * g + o
            p = self.place.xyz[(o + 1) % 3]

            @pl.when(p == g)
            def _():
                total = self.q_own[t]
                for slot in range(3):
                    self.second_copy(t, o, g, slot).wait_recv()
                    total = total + self.s_in[o, slot].astype(F32)
                self.t_buf[o, self.place.xyz[(o + 2) % 3]] = total.astype(BF)
                for d in (2, 1, 3):
                    self.third_copy(o, d).start()

    def step4(self, g):
        for o in range(3):
            t = 3 * g + o
            p = self.place.xyz[(o + 1) % 3]

            @pl.when(p == g)
            def _():
                for d in (1, 3, 2):
                    self.third_wait(o, d).wait_recv()
                buf = self.t_buf
                total = (buf[o, 0].astype(F32) + buf[o, 1].astype(F32)) + (buf[o, 2].astype(F32) + buf[o, 3].astype(F32))
                row = self.place.core * HALF + self.place.xyz[o] * QUART
                self.out[t, pl.ds(row, QUART)] = total.astype(BF)
                for d in (2, 1, 3):
                    self.gather2_copy(t, o, d).start()
                for d in (2, 1, 3):
                    self.gather1_copy(t, o, d).start()

    def step5(self, g):
        for o in range(3):
            t = 3 * g + o
            p = self.place.xyz[(o + 1) % 3]

            @pl.when(p != g)
            def _():
                self.gather2_copy(t, o, 1).wait_recv()
                for d in (2, 1, 3):
                    self.gather1_copy(t, o, d).start()

    def step6(self, g):
        for o in range(3):
            t = 3 * g + o
            for d in (1, 3, 2):
                self.gather1_wait(t, o, d).wait_recv()
            self.gatherc_copy(t).start()

    def step7(self, g):
        for o in range(3):
            self.gatherc_wait(3 * g + o).wait_recv()

    def sends(self, g):
        for o in range(3):
            t = 3 * g + o
            p = self.place.xyz[(o + 1) % 3]
            self.core_copy(t).wait_send()
            for d in (1, 2, 3):
                self.quarter_copy(t, o, d).wait_send()
                self.gather1_copy(t, o, d).wait_send()
            self.gatherc_copy(t).wait_send()

            @pl.when(p != g)
            def _():
                self.second_copy(t, o, g, (p + 4 - g) % 4 - 1).wait_send()

            @pl.when(p == g)
            def _():
                for d in (1, 2, 3):
                    self.third_copy(o, d).wait_send()
                    self.gather2_copy(t, o, d).wait_send()


def greet(place, halos):
    barrier = pltpu.get_barrier_semaphore()
    friends = [place.other()]
    for axis in range(3):
        for d in (1, 2, 3):
            friends.append(place.along(axis, (place.xyz[axis] + d) % 4))
    if halos:
        friends.append(((place.tm + 1) % 4, place.height))
        friends.append(((place.tm + 3) % 4, place.height))
        friends.append((place.tm, (place.height + 1) % 32))
        friends.append((place.tm, (place.height + 31) % 32))
    for device in friends:
        pl.semaphore_signal(barrier, inc=1, device_id=device, device_id_type=MESH)
    if halos:
        @pl.when(place.diagonal)
        def _():
            pl.semaphore_signal(barrier, inc=1, device_id=place.opposite, device_id_type=MESH)
            pl.semaphore_wait(barrier, len(friends) + 1)

        @pl.when(jnp.logical_not(place.diagonal))
        def _():
            pl.semaphore_wait(barrier, len(friends))
    else:
        pl.semaphore_wait(barrier, len(friends))


BOUNDS = (0, 176, 336, 496, 640)
CHUNKS = 4
CW = 160


def nt(left, right):
    return lax.dot_general(left, right, (((1,), (1,)), ((), ())), preferred_element_type=F32)


def tn(left, right):
    return lax.dot_general(left, right, (((0,), (0,)), ((), ())), preferred_element_type=F32)


def lanes(*values):
    return jnp.concatenate(values, axis=1)


def shifts(cot3, row, f, start, size):
    low, high = max(start - 16, 0), min(start + size + 16, 640)
    n = high - low
    for b in range(3):
        x = cot3[row, f, low:high, 384 + b * 128:384 + (b + 1) * 128].astype(F32)
        place = lax.broadcasted_iota(jnp.int32, (n, 128), 0)
        after = pltpu.roll(x, n - 1, 0)
        before = pltpu.roll(x, 1, 0)
        if high == 640:
            after = jnp.where(place == n - 1, 0.0, after)
        if low == 0:
            before = jnp.where(place == 0, 0.0, before)
        at = start - low
        cot3[row, f, start:start + size, b * 128:(b + 1) * 128] = after[at:at + size].astype(BF)
        cot3[row, f, start:start + size, 768 + b * 128:768 + (b + 1) * 128] = before[at:at + size].astype(BF)


def block_kernel(lat_hbm, cot_hbm, tw_hbm, sw_hbm, lg_hbm, tg_hbm, sg_hbm,
                 lat, cot3, back, hid, pgx, tw, twt, sw, part, out, lg,
                 in_sem, w_sem, l_sem, u_sem, d_sem, p_sem, o_sem, relay, r_sem, *refs):
    place = Place()
    tm, height = place.tm, place.height
    cot_in = [pltpu.make_async_copy(cot_hbm.at[:, r], cot3.at[r + 1, :, :, 384:768], in_sem.at[r]) for r in range(2)]
    lat_in = pltpu.make_async_copy(lat_hbm, lat.at[2:4], in_sem.at[2])
    tw_in = pltpu.make_async_copy(tw_hbm, tw, in_sem.at[3])
    sw_in = [pltpu.make_async_copy(sw_hbm.at[i, j], sw.at[i, :, j * 384:(j + 1) * 384], w_sem.at[3 * i + j])
             for i in (1, 0, 2) for j in range(3)]
    twt_in = [pltpu.make_async_copy(tw_hbm.at[k], twt.at[:, k * 384:(k + 1) * 384], w_sem.at[9 + k]) for k in range(3)]
    for copy in cot_in + sw_in + [lat_in, tw_in] + twt_in:
        copy.start()

    greet(place, True)

    def l_copy(c):
        cols = pl.ds(c * CW, CW)
        return remote(lat_hbm.at[:, :, cols], lat.at[0:2, :, cols], l_sem.at[c, 0], l_sem.at[c, 1],
                      ((tm + 1) % 4, height))

    def columns(c):
        return pl.ds(BOUNDS[c], BOUNDS[c + 1] - BOUNDS[c])

    def down_copy(c, f):
        cols = columns(c)
        return remote(cot_hbm.at[f, 1, cols], cot3.at[0, f, cols, 384:768], d_sem.at[c, f, 0], d_sem.at[c, f, 1],
                      (tm, (height + 1) % 32))

    def up_copy(c, f):
        cols = columns(c)
        return remote(cot_hbm.at[f, 0, cols], cot3.at[3, f, cols, 384:768], u_sem.at[c, f, 0], u_sem.at[c, f, 1],
                      (tm, (height + 31) % 32))

    x, y, z = place.xyz

    def slot(way, c, f):
        return relay.at[way, f, 0:BOUNDS[c + 1] - BOUNDS[c]]

    def to_relay(way, c, f):
        sem = (d_sem, u_sem)[way]
        device = (place.mirror, place.opposite, place.at(3 - x, y, z, place.core), place.at(x, y, 3 - z, place.core))[c]
        return remote(cot_hbm.at[f, 1 - way, columns(c)], slot(way, c, f), sem.at[c, f, 0], r_sem.at[way, f, 1], device)

    def to_mirror(way, c, f):
        return remote(slot(way, c, f), slot(way, c, f), r_sem.at[way, f, 0], r_sem.at[way, f, 1], place.mirror)

    def to_band(way, c, f):
        sem, row = ((d_sem, 0), (u_sem, 3))[way]
        device = (place.opposite, place.mirror, place.at(x, y, 3 - z, place.core), place.at(3 - x, y, z, place.core))[c]
        return remote(slot(way, c, f), cot3.at[row, f, columns(c), 384:768], r_sem.at[way, f, 0], sem.at[c, f, 1], device)

    def here(way, c):
        own = 3 - 3 * way
        column = ((x == own) & (z == own), (x == 3 - own) & (z == 3 - own), (x == 3 - own) & (z == own),
                  (x == own) & (z == 3 - own))[c]
        return place.corner & column

    def forward_first(f):
        for way in range(2):
            for c in range(1, 4):
                @pl.when(here(way, c) & (place.half == way))
                def _():
                    to_mirror(way, c, f).wait_recv()
                    (to_band if c == 1 else to_mirror)(way, c, f).start()

    def forward_second(f):
        for way in range(2):
            for c in (0, 2, 3):
                @pl.when(here(way, c) & (place.half == 1 - way))
                def _():
                    to_mirror(way, c, f).wait_recv()
                    to_band(way, c, f).start()

    def forward_sends(f):
        for way in range(2):
            for c in range(4):
                @pl.when(here(way, c) & (place.half == (1 - way if c == 0 else way)))
                def _():
                    to_mirror(way, c, f).wait_send()

            for c in (2, 3):
                @pl.when(here(way, c) & (place.half == 1 - way))
                def _():
                    to_mirror(way, c, f).wait_send()

    def p_copy(c):
        cols = pl.ds(c * CW, CW)
        return remote(pgx.at[0:2, :, cols], pgx.at[2:4, :, cols], p_sem.at[c, 0], p_sem.at[c, 1],
                      ((tm + 3) % 4, height))

    for c in range(CHUNKS):
        for f in range(2):
            @pl.when(height == 15)
            def _():
                to_relay(0, c, f).start()

            @pl.when(height == 16)
            def _():
                to_relay(1, c, f).start()

            @pl.when((height < 31) & (height != 15))
            def _():
                down_copy(c, f).start()

            @pl.when((height > 0) & (height != 16))
            def _():
                up_copy(c, f).start()

        @pl.when(tm < 3)
        def _():
            l_copy(c).start()

    @pl.when(tm == 0)
    def _():
        lat[0:2] = jnp.zeros((2, 2, 640, 384), BF)

    @pl.when(tm == 3)
    def _():
        pgx[2:4] = jnp.zeros((2, 2, 640, 384), BF)

    @pl.when(height == 0)
    def _():
        cot3[0, :, :, 384:768] = jnp.zeros((2, 640, 384), BF)

    @pl.when(height == 31)
    def _():
        cot3[3, :, :, 384:768] = jnp.zeros((2, 640, 384), BF)

    for copy in cot_in:
        copy.wait()
    for row in (1, 2):
        for f in range(2):
            shifts(cot3, row, f, 0, 640)
    for copy in sw_in:
        copy.wait()
    for f in range(2):
        back[0, f] = nt(lanes(cot3[1, f], cot3[2, f]), lanes(sw[1], sw[0]))
        forward_first(f)
        back[1, f] = nt(lanes(cot3[2, f], cot3[1, f]), lanes(sw[1], sw[2]))
    forward_second(0)
    lat_in.wait()
    tw_in.wait()
    for copy in twt_in:
        copy.wait()

    def add(g, lanes_of, half, value):
        part[g, :, lanes_of] = value if half == 0 else part[g, :, lanes_of] + value

    def spatial(i, half):
        cols = slice(half * 320, (half + 1) * 320)
        value = tn(hid[:, :, cols].reshape(1280, 384), cot3[2 - i:4 - i, :, cols].reshape(1280, 1152))
        add(i, slice(0, 1152), half, value)

    def temporal(half):
        cols = slice(half * 320, (half + 1) * 320)
        grads = pgx[0:2, :, cols].reshape(1280, 384)
        for k in range(3):
            value = tn(lat[2 - k:4 - k, :, cols].reshape(1280, 384), grads)
            add(3, slice(k * 384, (k + 1) * 384), half, value)

    weight = tw.reshape(1152, 384)
    for c in range(CHUNKS):
        cols = slice(c * CW, (c + 1) * CW)
        if c == 1:
            forward_second(1)

        @pl.when(tm > 0)
        def _():
            l_copy(c).wait_recv()

        factors = []
        for r in range(2):
            left = jnp.concatenate(
                [lanes(lat[f + 2, r, cols], lat[f + 1, r, cols], lat[f, r, cols]) for f in range(2)], axis=0)
            pre = jnp.dot(left, weight[...], preferred_element_type=F32)
            sigma = jax.nn.sigmoid(pre)
            hidden = (pre * sigma).astype(BF)
            for f in range(2):
                hid[r, f, cols] = hidden[f * CW:(f + 1) * CW]
            factors.append(sigma * (1.0 + pre * (1.0 - sigma)))
        for f in range(2):
            @pl.when(height > 0)
            def _():
                down_copy(c, f).wait_recv()

            @pl.when(height < 31)
            def _():
                up_copy(c, f).wait_recv()

        for row in (0, 3):
            for f in range(2):
                shifts(cot3, row, f, c * CW, CW)
        for r in range(2):
            halo, i = (0, 2) if r == 0 else (3, 0)
            window = jnp.concatenate([cot3[halo, f, cols] for f in range(2)], axis=0)
            total = nt(window, sw[i]) + jnp.concatenate([back[r, f, cols] for f in range(2)], axis=0)
            grad = (total * factors[r]).astype(BF)
            for f in range(2):
                pgx[f, r, cols] = grad[f * CW:(f + 1) * CW]

        @pl.when(tm > 0)
        def _():
            p_copy(c).start()

        if c == 1:
            for i in range(3):
                spatial(i, 0)
            temporal(0)

    red = Reduce(place, part, out, refs)

    def latent(f, r):
        grads = lanes(*(pgx[f + k, r] for k in range(3)))
        lg[f, r] = (cot3[r + 1, f, :, 384:768].astype(F32) + nt(grads, twt[...])).astype(BF)
        pltpu.make_async_copy(lg.at[f, r], lg_hbm.at[f, r], o_sem.at[4 + 2 * f + r]).start()

    def store(g):
        target = sg_hbm.at[g] if g < 3 else tg_hbm
        return pltpu.make_async_copy(out.at[3 * g:3 * g + 3], target, o_sem.at[g])

    def arrive():
        for c in range(CHUNKS):
            @pl.when(tm < 3)
            def _():
                p_copy(c).wait_recv()

    def last(g):
        red.step7(g)
        store(g).start()

    spatial(0, 1)
    red.step0(0)
    spatial(1, 1)
    red.step1(0)
    red.step0(1)
    spatial(2, 1)
    red.step1(1)
    red.step0(2)
    temporal(1)
    red.step1(2)
    red.step0(3)
    red.step2(0)
    red.step2(1)
    red.step1(3)
    red.step2(2)
    arrive()
    latent(0, 0)
    red.step2(3)
    latent(0, 1)
    red.step3(0)
    red.step3(1)
    red.step3(2)
    red.step3(3)
    latent(1, 0)
    red.step4(0)
    red.step4(1)
    red.step4(2)
    red.step4(3)
    latent(1, 1)
    red.step5(0)
    red.step5(1)
    red.step5(2)
    red.step5(3)
    red.step6(0)
    red.step6(1)
    red.step6(2)
    red.step6(3)
    last(0)
    last(1)
    last(2)
    last(3)

    for c in range(CHUNKS):
        @pl.when(tm < 3)
        def _():
            l_copy(c).wait_send()

        for f in range(2):
            @pl.when(height < 31)
            def _():
                down_copy(c, f).wait_send()

            @pl.when(height > 0)
            def _():
                up_copy(c, f).wait_send()

        @pl.when(tm > 0)
        def _():
            p_copy(c).wait_send()
    for f in range(2):
        forward_sends(f)
    for g in range(4):
        red.sends(g)
        store(g).wait()
    for f in range(2):
        for r in range(2):
            pltpu.make_async_copy(lg.at[f, r], lg_hbm.at[f, r], o_sem.at[4 + 2 * f + r]).wait()


def scale_kernel(scale, lg_ref, tg_ref, sg_ref, lg_out, tg_out, sg_out):
    lg_out[...] = lg_ref[...]
    tg_out[...] = tg_ref[...].astype(F32) * scale
    sg_out[...] = sg_ref[...].astype(F32) * scale


def scaled(latent_grad, temporal, spatial, scale):
    def blocks(rows):
        return pl.BlockSpec((rows // 4, 384), lambda i: (i, 0))

    latent_grad, temporal, spatial = pl.pallas_call(
        functools.partial(scale_kernel, scale),
        grid=(4,),
        out_shape=(
            jax.ShapeDtypeStruct((2560, 384), BF),
            jax.ShapeDtypeStruct((1152, 384), F32),
            jax.ShapeDtypeStruct((3456, 384), F32),
        ),
        in_specs=[blocks(2560), blocks(1152), blocks(3456)],
        out_specs=(blocks(2560), blocks(1152), blocks(3456)),
        compiler_params=pltpu.CompilerParams(vmem_limit_bytes=40 * 2**20),
    )(latent_grad.reshape(2560, 384), temporal.reshape(1152, 384), spatial.reshape(3456, 384))
    return latent_grad.reshape(2, 2, 640, 384), temporal.reshape(3, 384, 384), spatial.reshape(3, 3, 384, 384)


def on_device(latents, cotangent, temporal_weight, spatial_weight):
    frames, rows, cols, chans = latents.shape
    count = frames * lax.axis_size("tm") * rows * lax.axis_size("height") * cols
    scale = 1.0 / math.sqrt(count)
    anywhere = pl.BlockSpec(memory_space=pl.ANY)
    latent_grad, temporal, spatial = pl.pallas_call(
        block_kernel,
        out_shape=(
            jax.ShapeDtypeStruct((2, 2, 640, 384), BF),
            jax.ShapeDtypeStruct((3, 384, 384), BF),
            jax.ShapeDtypeStruct((3, 3, 384, 384), BF),
        ),
        in_specs=[anywhere] * 4,
        out_specs=(anywhere,) * 3,
        scratch_shapes=[
            pltpu.VMEM((4, 2, 640, 384), BF),
            pltpu.VMEM((4, 2, 640, 1152), BF),
            pltpu.VMEM((2, 2, 640, 384), F32),
            pltpu.VMEM((2, 2, 640, 384), BF),
            pltpu.VMEM((4, 2, 640, 384), BF),
            pltpu.VMEM((3, 384, 384), BF),
            pltpu.VMEM((384, 1152), BF),
            pltpu.VMEM((3, 384, 1152), BF),
            pltpu.VMEM((4, 384, 1152), F32),
            pltpu.VMEM((12, 384, 384), BF),
            pltpu.VMEM((2, 2, 640, 384), BF),
            pltpu.SemaphoreType.DMA((4,)),
            pltpu.SemaphoreType.DMA((12,)),
            pltpu.SemaphoreType.DMA((CHUNKS, 2)),
            pltpu.SemaphoreType.DMA((CHUNKS, 2, 2)),
            pltpu.SemaphoreType.DMA((CHUNKS, 2, 2)),
            pltpu.SemaphoreType.DMA((CHUNKS, 2)),
            pltpu.SemaphoreType.DMA((8,)),
            pltpu.VMEM((2, 2, 176, 384), BF),
            pltpu.SemaphoreType.DMA((2, 2, 2)),
        ] + Reduce.SCRATCH,
        compiler_params=pltpu.CompilerParams(
            collective_id=0, has_side_effects=True, vmem_limit_bytes=60 * 2**20),
    )(latents, cotangent, temporal_weight, spatial_weight)
    return scaled(latent_grad, temporal, spatial, scale)


def solution(mesh):
    return jax.shard_map(
        on_device,
        mesh=mesh,
        in_specs=(P("tm", "height", None, None), P("tm", "height", None, None), P(), P()),
        out_specs=(P("tm", "height", None, None), P(), P()),
        check_vma=False,
    )
```

```python
import functools
import math

import jax
import jax.numpy as jnp
from jax import lax
from jax.experimental import pallas as pl
from jax.experimental.pallas import tpu as pltpu
from jax.sharding import PartitionSpec as P

BF = jnp.bfloat16
F32 = jnp.float32
MESH = pl.DeviceIdType.MESH
HALF = 192
QUART = 48


class Place:
    def __init__(self):
        tm = lax.axis_index("tm")
        height = lax.axis_index("height")
        self.tm = tm
        self.height = height
        self.core = tm % 2
        self.xyz = (height % 4, (height // 16) * 2 + tm // 2, (height // 4) % 4)
        x, y, z = self.xyz
        self.corner = ((x == 0) | (x == 3)) & ((z == 0) | (z == 3))
        self.diagonal = self.corner & (x == z)
        self.half = height // 16
        self.mirror = self.at(x, (y + 2) % 4, z, self.core)
        self.opposite = self.at(3 - x, y, 3 - z, self.core)

    def at(self, x, y, z, core):
        return ((y % 2) * 2 + core, (y // 2) * 16 + z * 4 + x)

    def along(self, axis, where):
        xyz = list(self.xyz)
        xyz[axis] = where
        return self.at(*xyz, self.core)

    def other(self):
        return (self.tm + 1 - 2 * self.core, self.height)


def remote(src, dst, send, recv, device):
    return pltpu.make_async_remote_copy(
        src_ref=src, dst_ref=dst, send_sem=send, recv_sem=recv,
        device_id=device, device_id_type=MESH)


class Reduce:
    SCRATCH = [
        pltpu.VMEM((12, HALF, 384), BF),
        pltpu.VMEM((12, HALF, 384), BF),
        pltpu.VMEM((12, HALF, 384), BF),
        pltpu.VMEM((12, QUART, 384), F32),
        pltpu.VMEM((12, 3, QUART, 384), BF),
        pltpu.VMEM((12, QUART, 384), BF),
        pltpu.VMEM((3, 3, QUART, 384), BF),
        pltpu.VMEM((3, 4, QUART, 384), BF),
        pltpu.SemaphoreType.DMA((12, 2)),
        pltpu.SemaphoreType.DMA((12, 3, 2)),
        pltpu.SemaphoreType.DMA((12,)),
        pltpu.SemaphoreType.DMA((3, 3)),
        pltpu.SemaphoreType.DMA((3, 3, 2)),
        pltpu.SemaphoreType.DMA((3, 3)),
        pltpu.SemaphoreType.DMA((12,)),
        pltpu.SemaphoreType.DMA((12, 3, 2)),
        pltpu.SemaphoreType.DMA((12, 2)),
    ]

    def __init__(self, place, part, out, refs):
        self.place = place
        self.part = part
        self.out = out
        (self.c_out, self.c_in, self.q_out, self.q_own, self.q_in, self.s_out, self.s_in, self.t_buf,
         self.c_sem, self.q_sem, self.s_send, self.s_recv, self.t_sem, self.g2_send, self.g2_recv,
         self.g1_sem, self.gc_sem) = refs

    def core_copy(self, t):
        return remote(self.c_out.at[t], self.c_in.at[t], self.c_sem.at[t, 0], self.c_sem.at[t, 1], self.place.other())

    def quarter_copy(self, t, o, d):
        q = (self.place.xyz[o] + d) % 4
        return remote(self.q_out.at[t, pl.ds(q * QUART, QUART)], self.q_in.at[t, d - 1],
                      self.q_sem.at[t, d - 1, 0], self.q_sem.at[t, d - 1, 1], self.place.along(o, q))

    def second_copy(self, t, o, g, slot):
        b = (o + 1) % 3
        return remote(self.s_out.at[t], self.s_in.at[o, slot], self.s_send.at[t], self.s_recv.at[o, slot],
                      self.place.along(b, g))

    def third_copy(self, o, d):
        b = (o + 2) % 3
        p = self.place.xyz[b]
        return remote(self.t_buf.at[o, p], self.t_buf.at[o, p], self.t_sem.at[o, d - 1, 0], self.t_sem.at[o, d - 1, 1],
                      self.place.along(b, (p + d) % 4))

    def third_wait(self, o, d):
        p = (self.place.xyz[(o + 2) % 3] + 4 - d) % 4
        return remote(self.t_buf.at[o, p], self.t_buf.at[o, p], self.t_sem.at[o, d - 1, 0], self.t_sem.at[o, d - 1, 1],
                      self.place.other())

    def rows(self, t, q):
        return self.out.at[t, pl.ds(self.place.core * HALF + q * QUART, QUART)]

    def gather2_copy(self, t, o, d):
        b = (o + 1) % 3
        ref = self.rows(t, self.place.xyz[o])
        return remote(ref, ref, self.g2_send.at[o, d - 1], self.g2_recv.at[t],
                      self.place.along(b, (self.place.xyz[b] + d) % 4))

    def gather1_copy(self, t, o, d):
        p = self.place.xyz[o]
        ref = self.rows(t, p)
        return remote(ref, ref, self.g1_sem.at[t, d - 1, 0], self.g1_sem.at[t, d - 1, 1],
                      self.place.along(o, (p + d) % 4))

    def gather1_wait(self, t, o, d):
        ref = self.rows(t, (self.place.xyz[o] + 4 - d) % 4)
        return remote(ref, ref, self.g1_sem.at[t, d - 1, 0], self.g1_sem.at[t, d - 1, 1], self.place.other())

    def gatherc_copy(self, t):
        ref = self.out.at[t, pl.ds(self.place.core * HALF, HALF)]
        return remote(ref, ref, self.gc_sem.at[t, 0], self.gc_sem.at[t, 1], self.place.other())

    def gatherc_wait(self, t):
        ref = self.out.at[t, pl.ds((1 - self.place.core) * HALF, HALF)]
        return remote(ref, ref, self.gc_sem.at[t, 0], self.gc_sem.at[t, 1], self.place.other())

    def step0(self, g):
        for o in range(3):
            t = 3 * g + o
            self.c_out[t] = self.part[g, pl.ds((1 - self.place.core) * HALF, HALF), o * 384:(o + 1) * 384].astype(BF)
            self.core_copy(t).start()

    def step1(self, g):
        for o in range(3):
            t = 3 * g + o
            self.core_copy(t).wait_recv()
            mine = (g, pl.ds(self.place.core * HALF, HALF), slice(o * 384, (o + 1) * 384))
            total = self.part[mine] + self.c_in[t].astype(F32)
            self.part[mine] = total
            self.q_out[t] = total.astype(BF)
            for d in (2, 1, 3):
                self.quarter_copy(t, o, d).start()

    def step2(self, g):
        for o in range(3):
            t = 3 * g + o
            row = self.place.core * HALF + self.place.xyz[o] * QUART
            total = self.part[g, pl.ds(row, QUART), o * 384:(o + 1) * 384]
            for d in (1, 3, 2):
                self.quarter_copy(t, o, d).wait_recv()
                total = total + self.q_in[t, d - 1].astype(F32)
            self.q_own[t] = total
            self.s_out[t] = total.astype(BF)
            p = self.place.xyz[(o + 1) % 3]

            @pl.when(p != g)
            def _():
                self.second_copy(t, o, g, (p + 4 - g) % 4 - 1).start()

    def step3(self, g):
        for o in range(3):
            t = 3 * g + o
            p = self.place.xyz[(o + 1) % 3]

            @pl.when(p == g)
            def _():
                total = self.q_own[t]
                for slot in range(3):
                    self.second_copy(t, o, g, slot).wait_recv()
                    total = total + self.s_in[o, slot].astype(F32)
                self.t_buf[o, self.place.xyz[(o + 2) % 3]] = total.astype(BF)
                for d in (2, 1, 3):
                    self.third_copy(o, d).start()

    def step4(self, g):
        for o in range(3):
            t = 3 * g + o
            p = self.place.xyz[(o + 1) % 3]

            @pl.when(p == g)
            def _():
                for d in (1, 3, 2):
                    self.third_wait(o, d).wait_recv()
                buf = self.t_buf
                total = (buf[o, 0].astype(F32) + buf[o, 1].astype(F32)) + (buf[o, 2].astype(F32) + buf[o, 3].astype(F32))
                row = self.place.core * HALF + self.place.xyz[o] * QUART
                self.out[t, pl.ds(row, QUART)] = total.astype(BF)
                for d in (2, 1, 3):
                    self.gather2_copy(t, o, d).start()
                for d in (2, 1, 3):
                    self.gather1_copy(t, o, d).start()

    def step5(self, g):
        for o in range(3):
            t = 3 * g + o
            p = self.place.xyz[(o + 1) % 3]

            @pl.when(p != g)
            def _():
                self.gather2_copy(t, o, 1).wait_recv()
                for d in (2, 1, 3):
                    self.gather1_copy(t, o, d).start()

    def step6(self, g):
        for o in range(3):
            t = 3 * g + o
            for d in (1, 3, 2):
                self.gather1_wait(t, o, d).wait_recv()
            self.gatherc_copy(t).start()

    def step7(self, g):
        for o in range(3):
            self.gatherc_wait(3 * g + o).wait_recv()

    def sends(self, g):
        for o in range(3):
            t = 3 * g + o
            p = self.place.xyz[(o + 1) % 3]
            self.core_copy(t).wait_send()
            for d in (1, 2, 3):
                self.quarter_copy(t, o, d).wait_send()
                self.gather1_copy(t, o, d).wait_send()
            self.gatherc_copy(t).wait_send()

            @pl.when(p != g)
            def _():
                self.second_copy(t, o, g, (p + 4 - g) % 4 - 1).wait_send()

            @pl.when(p == g)
            def _():
                for d in (1, 2, 3):
                    self.third_copy(o, d).wait_send()
                    self.gather2_copy(t, o, d).wait_send()


def greet(place, halos):
    barrier = pltpu.get_barrier_semaphore()
    friends = [place.other()]
    for axis in range(3):
        for d in (1, 2, 3):
            friends.append(place.along(axis, (place.xyz[axis] + d) % 4))
    if halos:
        friends.append(((place.tm + 1) % 4, place.height))
        friends.append(((place.tm + 3) % 4, place.height))
        friends.append((place.tm, (place.height + 1) % 32))
        friends.append((place.tm, (place.height + 31) % 32))
    for device in friends:
        pl.semaphore_signal(barrier, inc=1, device_id=device, device_id_type=MESH)
    if halos:
        @pl.when(place.diagonal)
        def _():
            pl.semaphore_signal(barrier, inc=1, device_id=place.opposite, device_id_type=MESH)
            pl.semaphore_wait(barrier, len(friends) + 1)

        @pl.when(jnp.logical_not(place.diagonal))
        def _():
            pl.semaphore_wait(barrier, len(friends))
    else:
        pl.semaphore_wait(barrier, len(friends))


BOUNDS = (0, 176, 336, 496, 640)
CHUNKS = 4
CW = 160


def nt(left, right):
    return lax.dot_general(left, right, (((1,), (1,)), ((), ())), preferred_element_type=F32)


def tn(left, right):
    return lax.dot_general(left, right, (((0,), (0,)), ((), ())), preferred_element_type=F32)


def lanes(*values):
    return jnp.concatenate(values, axis=1)


def shifts(cot3, row, f, start, size):
    low, high = max(start - 16, 0), min(start + size + 16, 640)
    n = high - low
    for b in range(3):
        x = cot3[row, f, low:high, 384 + b * 128:384 + (b + 1) * 128].astype(F32)
        place = lax.broadcasted_iota(jnp.int32, (n, 128), 0)
        after = pltpu.roll(x, n - 1, 0)
        before = pltpu.roll(x, 1, 0)
        if high == 640:
            after = jnp.where(place == n - 1, 0.0, after)
        if low == 0:
            before = jnp.where(place == 0, 0.0, before)
        at = start - low
        cot3[row, f, start:start + size, b * 128:(b + 1) * 128] = after[at:at + size].astype(BF)
        cot3[row, f, start:start + size, 768 + b * 128:768 + (b + 1) * 128] = before[at:at + size].astype(BF)


def block_kernel(lat_hbm, cot_hbm, tw_hbm, sw_hbm, lg_hbm, tg_hbm, sg_hbm,
                 lat, cot3, back, hid, pgx, tw, twt, sw, part, out, lg,
                 in_sem, w_sem, l_sem, u_sem, d_sem, p_sem, o_sem, relay, r_sem, *refs):
    place = Place()
    tm, height = place.tm, place.height
    cot_in = [pltpu.make_async_copy(cot_hbm.at[:, r], cot3.at[r + 1, :, :, 384:768], in_sem.at[r]) for r in range(2)]
    lat_in = pltpu.make_async_copy(lat_hbm, lat.at[2:4], in_sem.at[2])
    tw_in = pltpu.make_async_copy(tw_hbm, tw, in_sem.at[3])
    sw_in = [pltpu.make_async_copy(sw_hbm.at[i, j], sw.at[i, :, j * 384:(j + 1) * 384], w_sem.at[3 * i + j])
             for i in (1, 0, 2) for j in range(3)]
    twt_in = [pltpu.make_async_copy(tw_hbm.at[k], twt.at[:, k * 384:(k + 1) * 384], w_sem.at[9 + k]) for k in range(3)]
    for copy in cot_in + sw_in + [lat_in, tw_in] + twt_in:
        copy.start()

    greet(place, True)

    def l_copy(c):
        cols = pl.ds(c * CW, CW)
        return remote(lat_hbm.at[:, :, cols], lat.at[0:2, :, cols], l_sem.at[c, 0], l_sem.at[c, 1],
                      ((tm + 1) % 4, height))

    def columns(c):
        return pl.ds(BOUNDS[c], BOUNDS[c + 1] - BOUNDS[c])

    def down_copy(c, f):
        cols = columns(c)
        return remote(cot_hbm.at[f, 1, cols], cot3.at[0, f, cols, 384:768], d_sem.at[c, f, 0], d_sem.at[c, f, 1],
                      (tm, (height + 1) % 32))

    def up_copy(c, f):
        cols = columns(c)
        return remote(cot_hbm.at[f, 0, cols], cot3.at[3, f, cols, 384:768], u_sem.at[c, f, 0], u_sem.at[c, f, 1],
                      (tm, (height + 31) % 32))

    x, y, z = place.xyz

    def slot(way, c, f):
        return relay.at[way, f, 0:BOUNDS[c + 1] - BOUNDS[c]]

    def to_relay(way, c, f):
        sem = (d_sem, u_sem)[way]
        device = (place.mirror, place.opposite, place.at(3 - x, y, z, place.core), place.at(x, y, 3 - z, place.core))[c]
        return remote(cot_hbm.at[f, 1 - way, columns(c)], slot(way, c, f), sem.at[c, f, 0], r_sem.at[way, f, 1], device)

    def to_mirror(way, c, f):
        return remote(slot(way, c, f), slot(way, c, f), r_sem.at[way, f, 0], r_sem.at[way, f, 1], place.mirror)

    def to_band(way, c, f):
        sem, row = ((d_sem, 0), (u_sem, 3))[way]
        device = (place.opposite, place.mirror, place.at(x, y, 3 - z, place.core), place.at(3 - x, y, z, place.core))[c]
        return remote(slot(way, c, f), cot3.at[row, f, columns(c), 384:768], r_sem.at[way, f, 0], sem.at[c, f, 1], device)

    def here(way, c):
        own = 3 - 3 * way
        column = ((x == own) & (z == own), (x == 3 - own) & (z == 3 - own), (x == 3 - own) & (z == own),
                  (x == own) & (z == 3 - own))[c]
        return place.corner & column

    def forward_first(f):
        for way in range(2):
            for c in range(1, 4):
                @pl.when(here(way, c) & (place.half == way))
                def _():
                    to_mirror(way, c, f).wait_recv()
                    (to_band if c == 1 else to_mirror)(way, c, f).start()

    def forward_second(f, chunks):
        for way in range(2):
            for c in chunks:
                @pl.when(here(way, c) & (place.half == 1 - way))
                def _():
                    to_mirror(way, c, f).wait_recv()
                    to_band(way, c, f).start()

    def forward_sends(f):
        for way in range(2):
            for c in range(4):
                @pl.when(here(way, c) & (place.half == (1 - way if c == 0 else way)))
                def _():
                    to_mirror(way, c, f).wait_send()

            for c in (2, 3):
                @pl.when(here(way, c) & (place.half == 1 - way))
                def _():
                    to_mirror(way, c, f).wait_send()

    def p_copy(c, f):
        cols = pl.ds(c * CW, CW)
        return remote(pgx.at[f, :, cols], pgx.at[f + 2, :, cols], p_sem.at[c, f, 0], p_sem.at[c, f, 1],
                      ((tm + 3) % 4, height))

    def give(c, f):
        @pl.when(tm > 0)
        def _():
            p_copy(c, f).start()

    for c in range(CHUNKS):
        for f in range(2):
            @pl.when(height == 15)
            def _():
                to_relay(0, c, f).start()

            @pl.when(height == 16)
            def _():
                to_relay(1, c, f).start()

            @pl.when((height < 31) & (height != 15))
            def _():
                down_copy(c, f).start()

            @pl.when((height > 0) & (height != 16))
            def _():
                up_copy(c, f).start()

        @pl.when(tm < 3)
        def _():
            l_copy(c).start()

    @pl.when(tm == 0)
    def _():
        lat[0:2] = jnp.zeros((2, 2, 640, 384), BF)

    @pl.when(tm == 3)
    def _():
        pgx[2:4] = jnp.zeros((2, 2, 640, 384), BF)

    @pl.when(height == 0)
    def _():
        cot3[0, :, :, 384:768] = jnp.zeros((2, 640, 384), BF)

    @pl.when(height == 31)
    def _():
        cot3[3, :, :, 384:768] = jnp.zeros((2, 640, 384), BF)

    for copy in cot_in:
        copy.wait()
    for row in (1, 2):
        for f in range(2):
            shifts(cot3, row, f, 0, 640)
    for copy in sw_in:
        copy.wait()
    for f in range(2):
        back[0, f] = nt(lanes(cot3[1, f], cot3[2, f]), lanes(sw[1], sw[0]))
        forward_first(f)
        back[1, f] = nt(lanes(cot3[2, f], cot3[1, f]), lanes(sw[1], sw[2]))
    lat_in.wait()
    tw_in.wait()
    for copy in twt_in:
        copy.wait()

    def add(g, lanes_of, half, value):
        part[g, :, lanes_of] = value if half == 0 else part[g, :, lanes_of] + value

    def spatial(i, half):
        cols = slice(half * 320, (half + 1) * 320)
        value = tn(hid[:, :, cols].reshape(1280, 384), cot3[2 - i:4 - i, :, cols].reshape(1280, 1152))
        add(i, slice(0, 1152), half, value)

    def temporal(half):
        cols = slice(half * 320, (half + 1) * 320)
        grads = pgx[0:2, :, cols].reshape(1280, 384)
        for k in range(3):
            value = tn(lat[2 - k:4 - k, :, cols].reshape(1280, 384), grads)
            add(3, slice(k * 384, (k + 1) * 384), half, value)

    weight = tw.reshape(1152, 384)
    def forward_part(c):
        cols = slice(c * CW, (c + 1) * CW)

        @pl.when(tm > 0)
        def _():
            l_copy(c).wait_recv()

        factors = []
        for r in range(2):
            left = jnp.concatenate(
                [lanes(lat[f + 2, r, cols], lat[f + 1, r, cols], lat[f, r, cols]) for f in range(2)], axis=0)
            pre = jnp.dot(left, weight[...], preferred_element_type=F32)
            sigma = jax.nn.sigmoid(pre)
            hidden = (pre * sigma).astype(BF)
            for f in range(2):
                hid[r, f, cols] = hidden[f * CW:(f + 1) * CW]
            factors.append(sigma * (1.0 + pre * (1.0 - sigma)))
        return factors

    def backward_part(c, factors):
        cols = slice(c * CW, (c + 1) * CW)
        for f in range(2):
            @pl.when(height > 0)
            def _():
                down_copy(c, f).wait_recv()

            @pl.when(height < 31)
            def _():
                up_copy(c, f).wait_recv()

        for row in (0, 3):
            for f in range(2):
                shifts(cot3, row, f, c * CW, CW)
        for r in range(2):
            halo, i = (0, 2) if r == 0 else (3, 0)
            window = jnp.concatenate([cot3[halo, f, cols] for f in range(2)], axis=0)
            total = nt(window, sw[i]) + jnp.concatenate([back[r, f, cols] for f in range(2)], axis=0)
            grad = (total * factors[r]).astype(BF)
            for f in range(2):
                pgx[f, r, cols] = grad[f * CW:(f + 1) * CW]

        for f in range(2):
            give(c, f)

    red = Reduce(place, part, out, refs)
    backward_part(0, forward_part(0))
    forward_second(0, (0,))
    backward_part(1, forward_part(1))
    forward_second(1, (0,))
    forward_second(0, (2, 3))
    spatial(0, 0)
    spatial(1, 0)
    forward_second(1, (2, 3))
    backward_part(2, forward_part(2))
    spatial(2, 0)
    temporal(0)
    backward_part(3, forward_part(3))

    def latent(f, r):
        grads = lanes(*(pgx[f + k, r] for k in range(3)))
        lg[f, r] = (cot3[r + 1, f, :, 384:768].astype(F32) + nt(grads, twt[...])).astype(BF)
        pltpu.make_async_copy(lg.at[f, r], lg_hbm.at[f, r], o_sem.at[4 + 2 * f + r]).start()

    def store(g):
        target = sg_hbm.at[g] if g < 3 else tg_hbm
        return pltpu.make_async_copy(out.at[3 * g:3 * g + 3], target, o_sem.at[g])

    def arrive():
        for c in range(CHUNKS):
            for f in range(2):
                @pl.when(tm < 3)
                def _():
                    p_copy(c, f).wait_recv()

    def last(g):
        red.step7(g)
        store(g).start()

    spatial(1, 1)
    red.step0(1)
    spatial(0, 1)
    red.step1(1)
    red.step0(0)
    spatial(2, 1)
    red.step0(2)
    red.step1(0)
    temporal(1)
    red.step1(2)
    red.step0(3)
    red.step2(0)
    red.step2(1)
    red.step1(3)
    red.step2(2)
    red.step2(3)
    red.step3(0)
    red.step3(1)
    red.step3(2)
    red.step3(3)
    red.step4(0)
    red.step4(1)
    red.step4(2)
    red.step4(3)
    red.step5(0)
    red.step5(1)
    red.step5(2)
    red.step5(3)
    arrive()
    latent(0, 0)
    latent(0, 1)
    latent(1, 0)
    red.step6(0)
    red.step6(1)
    red.step6(2)
    red.step6(3)
    latent(1, 1)
    last(0)
    last(1)
    last(2)
    last(3)

    for c in range(CHUNKS):
        @pl.when(tm < 3)
        def _():
            l_copy(c).wait_send()

        for f in range(2):
            @pl.when(height < 31)
            def _():
                down_copy(c, f).wait_send()

            @pl.when(height > 0)
            def _():
                up_copy(c, f).wait_send()

            @pl.when(tm > 0)
            def _():
                p_copy(c, f).wait_send()
    for f in range(2):
        forward_sends(f)
    for g in range(4):
        red.sends(g)
        store(g).wait()
    for f in range(2):
        for r in range(2):
            pltpu.make_async_copy(lg.at[f, r], lg_hbm.at[f, r], o_sem.at[4 + 2 * f + r]).wait()


def scale_kernel(scale, lg_ref, tg_ref, sg_ref, lg_out, tg_out, sg_out):
    lg_out[...] = lg_ref[...]
    tg_out[...] = tg_ref[...].astype(F32) * scale
    sg_out[...] = sg_ref[...].astype(F32) * scale


def scaled(latent_grad, temporal, spatial, scale):
    def blocks(rows):
        return pl.BlockSpec((rows // 4, 384), lambda i: (i, 0))

    latent_grad, temporal, spatial = pl.pallas_call(
        functools.partial(scale_kernel, scale),
        grid=(4,),
        out_shape=(
            jax.ShapeDtypeStruct((2560, 384), BF),
            jax.ShapeDtypeStruct((1152, 384), F32),
            jax.ShapeDtypeStruct((3456, 384), F32),
        ),
        in_specs=[blocks(2560), blocks(1152), blocks(3456)],
        out_specs=(blocks(2560), blocks(1152), blocks(3456)),
        compiler_params=pltpu.CompilerParams(vmem_limit_bytes=60 * 2**20),
    )(latent_grad.reshape(2560, 384), temporal.reshape(1152, 384), spatial.reshape(3456, 384))
    return latent_grad.reshape(2, 2, 640, 384), temporal.reshape(3, 384, 384), spatial.reshape(3, 3, 384, 384)


def on_device(latents, cotangent, temporal_weight, spatial_weight):
    frames, rows, cols, chans = latents.shape
    count = frames * lax.axis_size("tm") * rows * lax.axis_size("height") * cols
    scale = 1.0 / math.sqrt(count)
    anywhere = pl.BlockSpec(memory_space=pl.ANY)
    latent_grad, temporal, spatial = pl.pallas_call(
        block_kernel,
        out_shape=(
            jax.ShapeDtypeStruct((2, 2, 640, 384), BF),
            jax.ShapeDtypeStruct((3, 384, 384), BF),
            jax.ShapeDtypeStruct((3, 3, 384, 384), BF),
        ),
        in_specs=[anywhere] * 4,
        out_specs=(anywhere,) * 3,
        scratch_shapes=[
            pltpu.VMEM((4, 2, 640, 384), BF),
            pltpu.VMEM((4, 2, 640, 1152), BF),
            pltpu.VMEM((2, 2, 640, 384), F32),
            pltpu.VMEM((2, 2, 640, 384), BF),
            pltpu.VMEM((4, 2, 640, 384), BF),
            pltpu.VMEM((3, 384, 384), BF),
            pltpu.VMEM((384, 1152), BF),
            pltpu.VMEM((3, 384, 1152), BF),
            pltpu.VMEM((4, 384, 1152), F32),
            pltpu.VMEM((12, 384, 384), BF),
            pltpu.VMEM((2, 2, 640, 384), BF),
            pltpu.SemaphoreType.DMA((4,)),
            pltpu.SemaphoreType.DMA((12,)),
            pltpu.SemaphoreType.DMA((CHUNKS, 2)),
            pltpu.SemaphoreType.DMA((CHUNKS, 2, 2)),
            pltpu.SemaphoreType.DMA((CHUNKS, 2, 2)),
            pltpu.SemaphoreType.DMA((CHUNKS, 2, 2)),
            pltpu.SemaphoreType.DMA((8,)),
            pltpu.VMEM((2, 2, 176, 384), BF),
            pltpu.SemaphoreType.DMA((2, 2, 2)),
        ] + Reduce.SCRATCH,
        compiler_params=pltpu.CompilerParams(
            collective_id=0, has_side_effects=True, vmem_limit_bytes=60 * 2**20),
    )(latents, cotangent, temporal_weight, spatial_weight)
    return scaled(latent_grad, temporal, spatial, scale)


def solution(mesh):
    return jax.shard_map(
        on_device,
        mesh=mesh,
        in_specs=(P("tm", "height", None, None), P("tm", "height", None, None), P(), P()),
        out_specs=(P("tm", "height", None, None), P(), P()),
        check_vma=False,
    )
```

```python
import functools
import math

import jax
import jax.numpy as jnp
from jax import lax
from jax.experimental import pallas as pl
from jax.experimental.pallas import tpu as pltpu
from jax.sharding import PartitionSpec as P

BF = jnp.bfloat16
F32 = jnp.float32
MESH = pl.DeviceIdType.MESH
HALF = 192
QUART = 48


class Place:
    def __init__(self):
        tm = lax.axis_index("tm")
        height = lax.axis_index("height")
        self.tm = tm
        self.height = height
        self.core = tm % 2
        self.xyz = (height % 4, (height // 16) * 2 + tm // 2, (height // 4) % 4)
        x, y, z = self.xyz
        self.corner = ((x == 0) | (x == 3)) & ((z == 0) | (z == 3))
        self.diagonal = self.corner & (x == z)
        self.half = height // 16
        self.mirror = self.at(x, (y + 2) % 4, z, self.core)
        self.opposite = self.at(3 - x, y, 3 - z, self.core)

    def at(self, x, y, z, core):
        return ((y % 2) * 2 + core, (y // 2) * 16 + z * 4 + x)

    def along(self, axis, where):
        xyz = list(self.xyz)
        xyz[axis] = where
        return self.at(*xyz, self.core)

    def other(self):
        return (self.tm + 1 - 2 * self.core, self.height)


def remote(src, dst, send, recv, device):
    return pltpu.make_async_remote_copy(
        src_ref=src, dst_ref=dst, send_sem=send, recv_sem=recv,
        device_id=device, device_id_type=MESH)


class Reduce:
    SCRATCH = [
        pltpu.VMEM((12, HALF, 384), BF),
        pltpu.VMEM((12, HALF, 384), BF),
        pltpu.VMEM((12, HALF, 384), BF),
        pltpu.VMEM((12, QUART, 384), F32),
        pltpu.VMEM((12, 3, QUART, 384), BF),
        pltpu.VMEM((12, QUART, 384), BF),
        pltpu.VMEM((3, 3, QUART, 384), BF),
        pltpu.VMEM((3, 4, QUART, 384), BF),
        pltpu.SemaphoreType.DMA((12, 2)),
        pltpu.SemaphoreType.DMA((12, 3, 2)),
        pltpu.SemaphoreType.DMA((12,)),
        pltpu.SemaphoreType.DMA((3, 3)),
        pltpu.SemaphoreType.DMA((3, 3, 2)),
        pltpu.SemaphoreType.DMA((3, 3)),
        pltpu.SemaphoreType.DMA((12,)),
        pltpu.SemaphoreType.DMA((12, 3, 2)),
        pltpu.SemaphoreType.DMA((12, 2)),
    ]

    def __init__(self, place, part, out, refs):
        self.place = place
        self.part = part
        self.out = out
        (self.c_out, self.c_in, self.q_out, self.q_own, self.q_in, self.s_out, self.s_in, self.t_buf,
         self.c_sem, self.q_sem, self.s_send, self.s_recv, self.t_sem, self.g2_send, self.g2_recv,
         self.g1_sem, self.gc_sem) = refs

    def core_copy(self, t):
        return remote(self.c_out.at[t], self.c_in.at[t], self.c_sem.at[t, 0], self.c_sem.at[t, 1], self.place.other())

    def quarter_copy(self, t, o, d):
        q = (self.place.xyz[o] + d) % 4
        return remote(self.q_out.at[t, pl.ds(q * QUART, QUART)], self.q_in.at[t, d - 1],
                      self.q_sem.at[t, d - 1, 0], self.q_sem.at[t, d - 1, 1], self.place.along(o, q))

    def second_copy(self, t, o, g, slot):
        b = (o + 1) % 3
        return remote(self.s_out.at[t], self.s_in.at[o, slot], self.s_send.at[t], self.s_recv.at[o, slot],
                      self.place.along(b, g))

    def third_copy(self, o, d):
        b = (o + 2) % 3
        p = self.place.xyz[b]
        return remote(self.t_buf.at[o, p], self.t_buf.at[o, p], self.t_sem.at[o, d - 1, 0], self.t_sem.at[o, d - 1, 1],
                      self.place.along(b, (p + d) % 4))

    def third_wait(self, o, d):
        p = (self.place.xyz[(o + 2) % 3] + 4 - d) % 4
        return remote(self.t_buf.at[o, p], self.t_buf.at[o, p], self.t_sem.at[o, d - 1, 0], self.t_sem.at[o, d - 1, 1],
                      self.place.other())

    def rows(self, t, q):
        return self.out.at[t, pl.ds(self.place.core * HALF + q * QUART, QUART)]

    def gather2_copy(self, t, o, d):
        b = (o + 1) % 3
        ref = self.rows(t, self.place.xyz[o])
        return remote(ref, ref, self.g2_send.at[o, d - 1], self.g2_recv.at[t],
                      self.place.along(b, (self.place.xyz[b] + d) % 4))

    def gather1_copy(self, t, o, d):
        p = self.place.xyz[o]
        ref = self.rows(t, p)
        return remote(ref, ref, self.g1_sem.at[t, d - 1, 0], self.g1_sem.at[t, d - 1, 1],
                      self.place.along(o, (p + d) % 4))

    def gather1_wait(self, t, o, d):
        ref = self.rows(t, (self.place.xyz[o] + 4 - d) % 4)
        return remote(ref, ref, self.g1_sem.at[t, d - 1, 0], self.g1_sem.at[t, d - 1, 1], self.place.other())

    def gatherc_copy(self, t):
        ref = self.out.at[t, pl.ds(self.place.core * HALF, HALF)]
        return remote(ref, ref, self.gc_sem.at[t, 0], self.gc_sem.at[t, 1], self.place.other())

    def gatherc_wait(self, t):
        ref = self.out.at[t, pl.ds((1 - self.place.core) * HALF, HALF)]
        return remote(ref, ref, self.gc_sem.at[t, 0], self.gc_sem.at[t, 1], self.place.other())

    def step0(self, g):
        for o in range(3):
            t = 3 * g + o
            self.c_out[t] = self.part[g, pl.ds((1 - self.place.core) * HALF, HALF), o * 384:(o + 1) * 384].astype(BF)
            self.core_copy(t).start()

    def step1(self, g):
        for o in range(3):
            t = 3 * g + o
            self.core_copy(t).wait_recv()
            mine = (g, pl.ds(self.place.core * HALF, HALF), slice(o * 384, (o + 1) * 384))
            total = self.part[mine] + self.c_in[t].astype(F32)
            self.part[mine] = total
            self.q_out[t] = total.astype(BF)
            for d in (2, 1, 3):
                self.quarter_copy(t, o, d).start()

    def step2(self, g):
        for o in range(3):
            t = 3 * g + o
            row = self.place.core * HALF + self.place.xyz[o] * QUART
            total = self.part[g, pl.ds(row, QUART), o * 384:(o + 1) * 384]
            for d in (1, 3, 2):
                self.quarter_copy(t, o, d).wait_recv()
                total = total + self.q_in[t, d - 1].astype(F32)
            self.q_own[t] = total
            self.s_out[t] = total.astype(BF)
            p = self.place.xyz[(o + 1) % 3]

            @pl.when(p != g)
            def _():
                self.second_copy(t, o, g, (p + 4 - g) % 4 - 1).start()

    def step3(self, g):
        for o in range(3):
            t = 3 * g + o
            p = self.place.xyz[(o + 1) % 3]

            @pl.when(p == g)
            def _():
                total = self.q_own[t]
                for slot in range(3):
                    self.second_copy(t, o, g, slot).wait_recv()
                    total = total + self.s_in[o, slot].astype(F32)
                self.t_buf[o, self.place.xyz[(o + 2) % 3]] = total.astype(BF)
                for d in (2, 1, 3):
                    self.third_copy(o, d).start()

    def step4(self, g):
        for o in range(3):
            t = 3 * g + o
            p = self.place.xyz[(o + 1) % 3]

            @pl.when(p == g)
            def _():
                for d in (1, 3, 2):
                    self.third_wait(o, d).wait_recv()
                buf = self.t_buf
                total = (buf[o, 0].astype(F32) + buf[o, 1].astype(F32)) + (buf[o, 2].astype(F32) + buf[o, 3].astype(F32))
                row = self.place.core * HALF + self.place.xyz[o] * QUART
                self.out[t, pl.ds(row, QUART)] = total.astype(BF)
                for d in (2, 1, 3):
                    self.gather2_copy(t, o, d).start()
                for d in (2, 1, 3):
                    self.gather1_copy(t, o, d).start()

    def step5(self, g):
        for o in range(3):
            t = 3 * g + o
            p = self.place.xyz[(o + 1) % 3]

            @pl.when(p != g)
            def _():
                self.gather2_copy(t, o, 1).wait_recv()
                for d in (2, 1, 3):
                    self.gather1_copy(t, o, d).start()

    def step6(self, g):
        for o in range(3):
            t = 3 * g + o
            for d in (1, 3, 2):
                self.gather1_wait(t, o, d).wait_recv()
            self.gatherc_copy(t).start()

    def step7(self, g):
        for o in range(3):
            self.gatherc_wait(3 * g + o).wait_recv()

    def sends(self, g):
        for o in range(3):
            t = 3 * g + o
            p = self.place.xyz[(o + 1) % 3]
            self.core_copy(t).wait_send()
            for d in (1, 2, 3):
                self.quarter_copy(t, o, d).wait_send()
                self.gather1_copy(t, o, d).wait_send()
            self.gatherc_copy(t).wait_send()

            @pl.when(p != g)
            def _():
                self.second_copy(t, o, g, (p + 4 - g) % 4 - 1).wait_send()

            @pl.when(p == g)
            def _():
                for d in (1, 2, 3):
                    self.third_copy(o, d).wait_send()
                    self.gather2_copy(t, o, d).wait_send()


def greet(place, halos):
    barrier = pltpu.get_barrier_semaphore()
    friends = [place.other()]
    for axis in range(3):
        for d in (1, 2, 3):
            friends.append(place.along(axis, (place.xyz[axis] + d) % 4))
    if halos:
        friends.append(((place.tm + 1) % 4, place.height))
        friends.append(((place.tm + 3) % 4, place.height))
        friends.append((place.tm, (place.height + 1) % 32))
        friends.append((place.tm, (place.height + 31) % 32))
    for device in friends:
        pl.semaphore_signal(barrier, inc=1, device_id=device, device_id_type=MESH)
    if halos:
        @pl.when(place.diagonal)
        def _():
            pl.semaphore_signal(barrier, inc=1, device_id=place.opposite, device_id_type=MESH)
            pl.semaphore_wait(barrier, len(friends) + 1)

        @pl.when(jnp.logical_not(place.diagonal))
        def _():
            pl.semaphore_wait(barrier, len(friends))
    else:
        pl.semaphore_wait(barrier, len(friends))


BOUNDS = (0, 176, 336, 496, 640)
CHUNKS = 4
CW = 160


def nt(left, right):
    return lax.dot_general(left, right, (((1,), (1,)), ((), ())), preferred_element_type=F32)


def tn(left, right):
    return lax.dot_general(left, right, (((0,), (0,)), ((), ())), preferred_element_type=F32)


def lanes(*values):
    return jnp.concatenate(values, axis=1)


def shifts(cot3, row, f, start, size):
    low, high = max(start - 16, 0), min(start + size + 16, 640)
    n = high - low
    for b in range(3):
        x = cot3[row, f, low:high, 384 + b * 128:384 + (b + 1) * 128].astype(F32)
        place = lax.broadcasted_iota(jnp.int32, (n, 128), 0)
        after = pltpu.roll(x, n - 1, 0)
        before = pltpu.roll(x, 1, 0)
        if high == 640:
            after = jnp.where(place == n - 1, 0.0, after)
        if low == 0:
            before = jnp.where(place == 0, 0.0, before)
        at = start - low
        cot3[row, f, start:start + size, b * 128:(b + 1) * 128] = after[at:at + size].astype(BF)
        cot3[row, f, start:start + size, 768 + b * 128:768 + (b + 1) * 128] = before[at:at + size].astype(BF)


def block_kernel(lat_hbm, cot_hbm, tw_hbm, sw_hbm, lg_hbm, tg_hbm, sg_hbm,
                 lat, cot3, back, hid, pgx, tw, twt, sw, part, out, lg,
                 in_sem, w_sem, l_sem, u_sem, d_sem, p_sem, o_sem, relay, r_sem, *refs):
    place = Place()
    tm, height = place.tm, place.height
    cot_in = [pltpu.make_async_copy(cot_hbm.at[:, r], cot3.at[r + 1, :, :, 384:768], in_sem.at[r]) for r in range(2)]
    lat_in = pltpu.make_async_copy(lat_hbm, lat.at[2:4], in_sem.at[2])
    tw_in = pltpu.make_async_copy(tw_hbm, tw, in_sem.at[3])
    sw_in = [pltpu.make_async_copy(sw_hbm.at[i, j], sw.at[i, :, j * 384:(j + 1) * 384], w_sem.at[3 * i + j])
             for i in (1, 0, 2) for j in range(3)]
    twt_in = [pltpu.make_async_copy(tw_hbm.at[k], twt.at[:, k * 384:(k + 1) * 384], w_sem.at[9 + k]) for k in range(3)]
    for copy in cot_in + sw_in + [lat_in, tw_in] + twt_in:
        copy.start()

    greet(place, True)

    def l_copy(c):
        cols = pl.ds(c * CW, CW)
        return remote(lat_hbm.at[:, :, cols], lat.at[0:2, :, cols], l_sem.at[c, 0], l_sem.at[c, 1],
                      ((tm + 1) % 4, height))

    def columns(c):
        return pl.ds(BOUNDS[c], BOUNDS[c + 1] - BOUNDS[c])

    def down_copy(c, f):
        cols = columns(c)
        return remote(cot_hbm.at[f, 1, cols], cot3.at[0, f, cols, 384:768], d_sem.at[c, f, 0], d_sem.at[c, f, 1],
                      (tm, (height + 1) % 32))

    def up_copy(c, f):
        cols = columns(c)
        return remote(cot_hbm.at[f, 0, cols], cot3.at[3, f, cols, 384:768], u_sem.at[c, f, 0], u_sem.at[c, f, 1],
                      (tm, (height + 31) % 32))

    x, y, z = place.xyz

    def slot(way, c, f):
        return relay.at[way, f, 0:BOUNDS[c + 1] - BOUNDS[c]]

    def to_relay(way, c, f):
        sem = (d_sem, u_sem)[way]
        device = (place.mirror, place.opposite, place.at(3 - x, y, z, place.core), place.at(x, y, 3 - z, place.core))[c]
        return remote(cot_hbm.at[f, 1 - way, columns(c)], slot(way, c, f), sem.at[c, f, 0], r_sem.at[way, f, 1], device)

    def to_mirror(way, c, f):
        return remote(slot(way, c, f), slot(way, c, f), r_sem.at[way, f, 0], r_sem.at[way, f, 1], place.mirror)

    def to_band(way, c, f):
        sem, row = ((d_sem, 0), (u_sem, 3))[way]
        device = (place.opposite, place.mirror, place.at(x, y, 3 - z, place.core), place.at(3 - x, y, z, place.core))[c]
        return remote(slot(way, c, f), cot3.at[row, f, columns(c), 384:768], r_sem.at[way, f, 0], sem.at[c, f, 1], device)

    def here(way, c):
        own = 3 - 3 * way
        column = ((x == own) & (z == own), (x == 3 - own) & (z == 3 - own), (x == 3 - own) & (z == own),
                  (x == own) & (z == 3 - own))[c]
        return place.corner & column

    def forward_first(f):
        for way in range(2):
            for c in range(1, 4):
                @pl.when(here(way, c) & (place.half == way))
                def _():
                    to_mirror(way, c, f).wait_recv()
                    (to_band if c == 1 else to_mirror)(way, c, f).start()

    def forward_second(f):
        for way in range(2):
            for c in (0, 2, 3):
                @pl.when(here(way, c) & (place.half == 1 - way))
                def _():
                    to_mirror(way, c, f).wait_recv()
                    to_band(way, c, f).start()

    def forward_sends(f):
        for way in range(2):
            for c in range(4):
                @pl.when(here(way, c) & (place.half == (1 - way if c == 0 else way)))
                def _():
                    to_mirror(way, c, f).wait_send()

            for c in (2, 3):
                @pl.when(here(way, c) & (place.half == 1 - way))
                def _():
                    to_mirror(way, c, f).wait_send()

    def p_copy(c):
        cols = pl.ds(c * CW, CW)
        return remote(pgx.at[0:2, :, cols], pgx.at[2:4, :, cols], p_sem.at[c, 0], p_sem.at[c, 1],
                      ((tm + 3) % 4, height))

    for c in range(CHUNKS):
        for f in range(2):
            @pl.when(height == 15)
            def _():
                to_relay(0, c, f).start()

            @pl.when(height == 16)
            def _():
                to_relay(1, c, f).start()

            @pl.when((height < 31) & (height != 15))
            def _():
                down_copy(c, f).start()

            @pl.when((height > 0) & (height != 16))
            def _():
                up_copy(c, f).start()

        @pl.when(tm < 3)
        def _():
            l_copy(c).start()

    @pl.when(tm == 0)
    def _():
        lat[0:2] = jnp.zeros((2, 2, 640, 384), BF)

    @pl.when(tm == 3)
    def _():
        pgx[2:4] = jnp.zeros((2, 2, 640, 384), BF)

    @pl.when(height == 0)
    def _():
        cot3[0, :, :, 384:768] = jnp.zeros((2, 640, 384), BF)

    @pl.when(height == 31)
    def _():
        cot3[3, :, :, 384:768] = jnp.zeros((2, 640, 384), BF)

    for copy in cot_in:
        copy.wait()
    for row in (1, 2):
        for f in range(2):
            shifts(cot3, row, f, 0, 640)
    for copy in sw_in:
        copy.wait()
    for f in range(2):
        back[0, f] = nt(lanes(cot3[1, f], cot3[2, f]), lanes(sw[1], sw[0]))
        forward_first(f)
        back[1, f] = nt(lanes(cot3[2, f], cot3[1, f]), lanes(sw[1], sw[2]))
    forward_second(0)
    lat_in.wait()
    tw_in.wait()
    for copy in twt_in:
        copy.wait()

    def add(g, lanes_of, half, value):
        part[g, :, lanes_of] = value if half == 0 else part[g, :, lanes_of] + value

    def spatial(i, half):
        cols = slice(half * 320, (half + 1) * 320)
        value = tn(hid[:, :, cols].reshape(1280, 384), cot3[2 - i:4 - i, :, cols].reshape(1280, 1152))
        add(i, slice(0, 1152), half, value)

    def temporal(half):
        cols = slice(half * 320, (half + 1) * 320)
        grads = pgx[0:2, :, cols].reshape(1280, 384)
        for k in range(3):
            value = tn(lat[2 - k:4 - k, :, cols].reshape(1280, 384), grads)
            add(3, slice(k * 384, (k + 1) * 384), half, value)

    weight = tw.reshape(1152, 384)
    def forward_part(c):
        cols = slice(c * CW, (c + 1) * CW)

        @pl.when(tm > 0)
        def _():
            l_copy(c).wait_recv()

        factors = []
        for r in range(2):
            left = jnp.concatenate(
                [lanes(lat[f + 2, r, cols], lat[f + 1, r, cols], lat[f, r, cols]) for f in range(2)], axis=0)
            pre = jnp.dot(left, weight[...], preferred_element_type=F32)
            sigma = jax.nn.sigmoid(pre)
            hidden = (pre * sigma).astype(BF)
            for f in range(2):
                hid[r, f, cols] = hidden[f * CW:(f + 1) * CW]
            factors.append(sigma * (1.0 + pre * (1.0 - sigma)))
        return factors

    def backward_part(c, factors):
        cols = slice(c * CW, (c + 1) * CW)
        for f in range(2):
            @pl.when(height > 0)
            def _():
                down_copy(c, f).wait_recv()

            @pl.when(height < 31)
            def _():
                up_copy(c, f).wait_recv()

        for row in (0, 3):
            for f in range(2):
                shifts(cot3, row, f, c * CW, CW)
        for r in range(2):
            halo, i = (0, 2) if r == 0 else (3, 0)
            window = jnp.concatenate([cot3[halo, f, cols] for f in range(2)], axis=0)
            total = nt(window, sw[i]) + jnp.concatenate([back[r, f, cols] for f in range(2)], axis=0)
            grad = (total * factors[r]).astype(BF)
            for f in range(2):
                pgx[f, r, cols] = grad[f * CW:(f + 1) * CW]

        @pl.when(tm > 0)
        def _():
            p_copy(c).start()

    red = Reduce(place, part, out, refs)
    backward_part(0, forward_part(0))
    forward_second(1)
    backward_part(1, forward_part(1))
    for i in range(3):
        spatial(i, 0)
    temporal(0)
    factors = [forward_part(c) for c in (2, 3)]
    spatial(1, 1)
    red.step0(1)
    for c in (2, 3):
        backward_part(c, factors[c - 2])

    def latent(f, r):
        grads = lanes(*(pgx[f + k, r] for k in range(3)))
        lg[f, r] = (cot3[r + 1, f, :, 384:768].astype(F32) + nt(grads, twt[...])).astype(BF)
        pltpu.make_async_copy(lg.at[f, r], lg_hbm.at[f, r], o_sem.at[4 + 2 * f + r]).start()

    def store(g):
        target = sg_hbm.at[g] if g < 3 else tg_hbm
        return pltpu.make_async_copy(out.at[3 * g:3 * g + 3], target, o_sem.at[g])

    def arrive():
        for c in range(CHUNKS):
            @pl.when(tm < 3)
            def _():
                p_copy(c).wait_recv()

    def last(g):
        red.step7(g)
        store(g).start()

    spatial(0, 1)
    red.step0(0)
    red.step1(1)
    spatial(2, 1)
    red.step0(2)
    red.step1(0)
    temporal(1)
    red.step1(2)
    red.step0(3)
    red.step2(0)
    red.step2(1)
    red.step1(3)
    red.step2(2)
    red.step2(3)
    red.step3(0)
    red.step3(1)
    red.step3(2)
    red.step3(3)
    red.step4(0)
    red.step4(1)
    red.step4(2)
    red.step4(3)
    red.step5(0)
    red.step5(1)
    red.step5(2)
    red.step5(3)
    arrive()
    latent(0, 0)
    latent(0, 1)
    latent(1, 0)
    red.step6(0)
    red.step6(1)
    red.step6(2)
    red.step6(3)
    latent(1, 1)
    last(0)
    last(1)
    last(2)
    last(3)

    for c in range(CHUNKS):
        @pl.when(tm < 3)
        def _():
            l_copy(c).wait_send()

        for f in range(2):
            @pl.when(height < 31)
            def _():
                down_copy(c, f).wait_send()

            @pl.when(height > 0)
            def _():
                up_copy(c, f).wait_send()

        @pl.when(tm > 0)
        def _():
            p_copy(c).wait_send()
    for f in range(2):
        forward_sends(f)
    for g in range(4):
        red.sends(g)
        store(g).wait()
    for f in range(2):
        for r in range(2):
            pltpu.make_async_copy(lg.at[f, r], lg_hbm.at[f, r], o_sem.at[4 + 2 * f + r]).wait()


def scale_kernel(scale, lg_ref, tg_ref, sg_ref, lg_out, tg_out, sg_out):
    lg_out[...] = lg_ref[...]
    tg_out[...] = tg_ref[...].astype(F32) * scale
    sg_out[...] = sg_ref[...].astype(F32) * scale


def scaled(latent_grad, temporal, spatial, scale):
    def blocks(rows):
        return pl.BlockSpec((rows // 4, 384), lambda i: (i, 0))

    latent_grad, temporal, spatial = pl.pallas_call(
        functools.partial(scale_kernel, scale),
        grid=(4,),
        out_shape=(
            jax.ShapeDtypeStruct((2560, 384), BF),
            jax.ShapeDtypeStruct((1152, 384), F32),
            jax.ShapeDtypeStruct((3456, 384), F32),
        ),
        in_specs=[blocks(2560), blocks(1152), blocks(3456)],
        out_specs=(blocks(2560), blocks(1152), blocks(3456)),
        compiler_params=pltpu.CompilerParams(vmem_limit_bytes=60 * 2**20),
    )(latent_grad.reshape(2560, 384), temporal.reshape(1152, 384), spatial.reshape(3456, 384))
    return latent_grad.reshape(2, 2, 640, 384), temporal.reshape(3, 384, 384), spatial.reshape(3, 3, 384, 384)


def on_device(latents, cotangent, temporal_weight, spatial_weight):
    frames, rows, cols, chans = latents.shape
    count = frames * lax.axis_size("tm") * rows * lax.axis_size("height") * cols
    scale = 1.0 / math.sqrt(count)
    anywhere = pl.BlockSpec(memory_space=pl.ANY)
    latent_grad, temporal, spatial = pl.pallas_call(
        block_kernel,
        out_shape=(
            jax.ShapeDtypeStruct((2, 2, 640, 384), BF),
            jax.ShapeDtypeStruct((3, 384, 384), BF),
            jax.ShapeDtypeStruct((3, 3, 384, 384), BF),
        ),
        in_specs=[anywhere] * 4,
        out_specs=(anywhere,) * 3,
        scratch_shapes=[
            pltpu.VMEM((4, 2, 640, 384), BF),
            pltpu.VMEM((4, 2, 640, 1152), BF),
            pltpu.VMEM((2, 2, 640, 384), F32),
            pltpu.VMEM((2, 2, 640, 384), BF),
            pltpu.VMEM((4, 2, 640, 384), BF),
            pltpu.VMEM((3, 384, 384), BF),
            pltpu.VMEM((384, 1152), BF),
            pltpu.VMEM((3, 384, 1152), BF),
            pltpu.VMEM((4, 384, 1152), F32),
            pltpu.VMEM((12, 384, 384), BF),
            pltpu.VMEM((2, 2, 640, 384), BF),
            pltpu.SemaphoreType.DMA((4,)),
            pltpu.SemaphoreType.DMA((12,)),
            pltpu.SemaphoreType.DMA((CHUNKS, 2)),
            pltpu.SemaphoreType.DMA((CHUNKS, 2, 2)),
            pltpu.SemaphoreType.DMA((CHUNKS, 2, 2)),
            pltpu.SemaphoreType.DMA((CHUNKS, 2)),
            pltpu.SemaphoreType.DMA((8,)),
            pltpu.VMEM((2, 2, 176, 384), BF),
            pltpu.SemaphoreType.DMA((2, 2, 2)),
        ] + Reduce.SCRATCH,
        compiler_params=pltpu.CompilerParams(
            collective_id=0, has_side_effects=True, vmem_limit_bytes=60 * 2**20),
    )(latents, cotangent, temporal_weight, spatial_weight)
    return scaled(latent_grad, temporal, spatial, scale)


def solution(mesh):
    return jax.shard_map(
        on_device,
        mesh=mesh,
        in_specs=(P("tm", "height", None, None), P("tm", "height", None, None), P(), P()),
        out_specs=(P("tm", "height", None, None), P(), P()),
        check_vma=False,
    )
```

```python
import functools
import math

import jax
import jax.numpy as jnp
from jax import lax
from jax.experimental import pallas as pl
from jax.experimental.pallas import tpu as pltpu
from jax.sharding import PartitionSpec as P

BF = jnp.bfloat16
F32 = jnp.float32
MESH = pl.DeviceIdType.MESH
HALF = 192
QUART = 48


class Place:
    def __init__(self):
        tm = lax.axis_index("tm")
        height = lax.axis_index("height")
        self.tm = tm
        self.height = height
        self.core = tm % 2
        self.xyz = (height % 4, (height // 16) * 2 + tm // 2, (height // 4) % 4)
        x, y, z = self.xyz
        self.corner = ((x == 0) | (x == 3)) & ((z == 0) | (z == 3))
        self.diagonal = self.corner & (x == z)
        self.half = height // 16
        self.mirror = self.at(x, (y + 2) % 4, z, self.core)
        self.opposite = self.at(3 - x, y, 3 - z, self.core)

    def at(self, x, y, z, core):
        return ((y % 2) * 2 + core, (y // 2) * 16 + z * 4 + x)

    def along(self, axis, where):
        xyz = list(self.xyz)
        xyz[axis] = where
        return self.at(*xyz, self.core)

    def other(self):
        return (self.tm + 1 - 2 * self.core, self.height)


def remote(src, dst, send, recv, device):
    return pltpu.make_async_remote_copy(
        src_ref=src, dst_ref=dst, send_sem=send, recv_sem=recv,
        device_id=device, device_id_type=MESH)


class Reduce:
    SCRATCH = [
        pltpu.VMEM((12, HALF, 384), BF),
        pltpu.VMEM((12, HALF, 384), BF),
        pltpu.VMEM((12, HALF, 384), BF),
        pltpu.VMEM((12, QUART, 384), F32),
        pltpu.VMEM((12, 3, QUART, 384), BF),
        pltpu.VMEM((12, QUART, 384), BF),
        pltpu.VMEM((3, 3, QUART, 384), BF),
        pltpu.VMEM((3, 4, QUART, 384), BF),
        pltpu.SemaphoreType.DMA((12, 2)),
        pltpu.SemaphoreType.DMA((12, 3, 2)),
        pltpu.SemaphoreType.DMA((12,)),
        pltpu.SemaphoreType.DMA((3, 3)),
        pltpu.SemaphoreType.DMA((3, 3, 2)),
        pltpu.SemaphoreType.DMA((3, 3)),
        pltpu.SemaphoreType.DMA((12,)),
        pltpu.SemaphoreType.DMA((12, 3, 2)),
        pltpu.SemaphoreType.DMA((12, 2)),
    ]

    def __init__(self, place, part, out, refs):
        self.place = place
        self.part = part
        self.out = out
        (self.c_out, self.c_in, self.q_out, self.q_own, self.q_in, self.s_out, self.s_in, self.t_buf,
         self.c_sem, self.q_sem, self.s_send, self.s_recv, self.t_sem, self.g2_send, self.g2_recv,
         self.g1_sem, self.gc_sem) = refs

    def core_copy(self, t):
        return remote(self.c_out.at[t], self.c_in.at[t], self.c_sem.at[t, 0], self.c_sem.at[t, 1], self.place.other())

    def quarter_copy(self, t, o, d):
        q = (self.place.xyz[o] + d) % 4
        return remote(self.q_out.at[t, pl.ds(q * QUART, QUART)], self.q_in.at[t, d - 1],
                      self.q_sem.at[t, d - 1, 0], self.q_sem.at[t, d - 1, 1], self.place.along(o, q))

    def second_copy(self, t, o, g, slot):
        b = (o + 1) % 3
        return remote(self.s_out.at[t], self.s_in.at[o, slot], self.s_send.at[t], self.s_recv.at[o, slot],
                      self.place.along(b, g))

    def third_copy(self, o, d):
        b = (o + 2) % 3
        p = self.place.xyz[b]
        return remote(self.t_buf.at[o, p], self.t_buf.at[o, p], self.t_sem.at[o, d - 1, 0], self.t_sem.at[o, d - 1, 1],
                      self.place.along(b, (p + d) % 4))

    def third_wait(self, o, d):
        p = (self.place.xyz[(o + 2) % 3] + 4 - d) % 4
        return remote(self.t_buf.at[o, p], self.t_buf.at[o, p], self.t_sem.at[o, d - 1, 0], self.t_sem.at[o, d - 1, 1],
                      self.place.other())

    def rows(self, t, q):
        return self.out.at[t, pl.ds(self.place.core * HALF + q * QUART, QUART)]

    def gather2_copy(self, t, o, d):
        b = (o + 1) % 3
        ref = self.rows(t, self.place.xyz[o])
        return remote(ref, ref, self.g2_send.at[o, d - 1], self.g2_recv.at[t],
                      self.place.along(b, (self.place.xyz[b] + d) % 4))

    def gather1_copy(self, t, o, d):
        p = self.place.xyz[o]
        ref = self.rows(t, p)
        return remote(ref, ref, self.g1_sem.at[t, d - 1, 0], self.g1_sem.at[t, d - 1, 1],
                      self.place.along(o, (p + d) % 4))

    def gather1_wait(self, t, o, d):
        ref = self.rows(t, (self.place.xyz[o] + 4 - d) % 4)
        return remote(ref, ref, self.g1_sem.at[t, d - 1, 0], self.g1_sem.at[t, d - 1, 1], self.place.other())

    def gatherc_copy(self, t):
        ref = self.out.at[t, pl.ds(self.place.core * HALF, HALF)]
        return remote(ref, ref, self.gc_sem.at[t, 0], self.gc_sem.at[t, 1], self.place.other())

    def gatherc_wait(self, t):
        ref = self.out.at[t, pl.ds((1 - self.place.core) * HALF, HALF)]
        return remote(ref, ref, self.gc_sem.at[t, 0], self.gc_sem.at[t, 1], self.place.other())

    def step0(self, g):
        for o in range(3):
            t = 3 * g + o
            self.c_out[t] = self.part[g, pl.ds((1 - self.place.core) * HALF, HALF), o * 384:(o + 1) * 384].astype(BF)
            self.core_copy(t).start()

    def step1(self, g):
        for o in range(3):
            t = 3 * g + o
            self.core_copy(t).wait_recv()
            mine = (g, pl.ds(self.place.core * HALF, HALF), slice(o * 384, (o + 1) * 384))
            total = self.part[mine] + self.c_in[t].astype(F32)
            self.part[mine] = total
            self.q_out[t] = total.astype(BF)
            for d in (2, 1, 3):
                self.quarter_copy(t, o, d).start()

    def step2(self, g):
        for o in range(3):
            t = 3 * g + o
            row = self.place.core * HALF + self.place.xyz[o] * QUART
            total = self.part[g, pl.ds(row, QUART), o * 384:(o + 1) * 384]
            for d in (1, 3, 2):
                self.quarter_copy(t, o, d).wait_recv()
                total = total + self.q_in[t, d - 1].astype(F32)
            self.q_own[t] = total
            self.s_out[t] = total.astype(BF)
            p = self.place.xyz[(o + 1) % 3]

            @pl.when(p != g)
            def _():
                self.second_copy(t, o, g, (p + 4 - g) % 4 - 1).start()

    def step3(self, g):
        for o in range(3):
            t = 3 * g + o
            p = self.place.xyz[(o + 1) % 3]

            @pl.when(p == g)
            def _():
                total = self.q_own[t]
                for slot in range(3):
                    self.second_copy(t, o, g, slot).wait_recv()
                    total = total + self.s_in[o, slot].astype(F32)
                self.t_buf[o, self.place.xyz[(o + 2) % 3]] = total.astype(BF)
                for d in (2, 1, 3):
                    self.third_copy(o, d).start()

    def step4(self, g):
        for o in range(3):
            t = 3 * g + o
            p = self.place.xyz[(o + 1) % 3]

            @pl.when(p == g)
            def _():
                for d in (1, 3, 2):
                    self.third_wait(o, d).wait_recv()
                buf = self.t_buf
                total = (buf[o, 0].astype(F32) + buf[o, 1].astype(F32)) + (buf[o, 2].astype(F32) + buf[o, 3].astype(F32))
                row = self.place.core * HALF + self.place.xyz[o] * QUART
                self.out[t, pl.ds(row, QUART)] = total.astype(BF)
                for d in (2, 1, 3):
                    self.gather2_copy(t, o, d).start()
                for d in (2, 1, 3):
                    self.gather1_copy(t, o, d).start()

    def step5(self, g):
        for o in range(3):
            t = 3 * g + o
            p = self.place.xyz[(o + 1) % 3]

            @pl.when(p != g)
            def _():
                self.gather2_copy(t, o, 1).wait_recv()
                for d in (2, 1, 3):
                    self.gather1_copy(t, o, d).start()

    def step6(self, g):
        for o in range(3):
            t = 3 * g + o
            for d in (1, 3, 2):
                self.gather1_wait(t, o, d).wait_recv()
            self.gatherc_copy(t).start()

    def step7(self, g):
        for o in range(3):
            self.gatherc_wait(3 * g + o).wait_recv()

    def sends(self, g):
        for o in range(3):
            t = 3 * g + o
            p = self.place.xyz[(o + 1) % 3]
            self.core_copy(t).wait_send()
            for d in (1, 2, 3):
                self.quarter_copy(t, o, d).wait_send()
                self.gather1_copy(t, o, d).wait_send()
            self.gatherc_copy(t).wait_send()

            @pl.when(p != g)
            def _():
                self.second_copy(t, o, g, (p + 4 - g) % 4 - 1).wait_send()

            @pl.when(p == g)
            def _():
                for d in (1, 2, 3):
                    self.third_copy(o, d).wait_send()
                    self.gather2_copy(t, o, d).wait_send()


def greet(place, halos):
    barrier = pltpu.get_barrier_semaphore()
    friends = [place.other()]
    for axis in range(3):
        for d in (1, 2, 3):
            friends.append(place.along(axis, (place.xyz[axis] + d) % 4))
    if halos:
        friends.append(((place.tm + 1) % 4, place.height))
        friends.append(((place.tm + 3) % 4, place.height))
        friends.append((place.tm, (place.height + 1) % 32))
        friends.append((place.tm, (place.height + 31) % 32))
    for device in friends:
        pl.semaphore_signal(barrier, inc=1, device_id=device, device_id_type=MESH)
    if halos:
        @pl.when(place.diagonal)
        def _():
            pl.semaphore_signal(barrier, inc=1, device_id=place.opposite, device_id_type=MESH)
            pl.semaphore_wait(barrier, len(friends) + 1)

        @pl.when(jnp.logical_not(place.diagonal))
        def _():
            pl.semaphore_wait(barrier, len(friends))
    else:
        pl.semaphore_wait(barrier, len(friends))


BOUNDS = (0, 176, 336, 496, 640)
CHUNKS = 4
CW = 160


def nt(left, right):
    return lax.dot_general(left, right, (((1,), (1,)), ((), ())), preferred_element_type=F32)


def tn(left, right):
    return lax.dot_general(left, right, (((0,), (0,)), ((), ())), preferred_element_type=F32)


def lanes(*values):
    return jnp.concatenate(values, axis=1)


def shifts(cot3, row, f, start, size):
    low, high = max(start - 16, 0), min(start + size + 16, 640)
    n = high - low
    for b in range(3):
        x = cot3[row, f, low:high, 384 + b * 128:384 + (b + 1) * 128].astype(F32)
        place = lax.broadcasted_iota(jnp.int32, (n, 128), 0)
        after = pltpu.roll(x, n - 1, 0)
        before = pltpu.roll(x, 1, 0)
        if high == 640:
            after = jnp.where(place == n - 1, 0.0, after)
        if low == 0:
            before = jnp.where(place == 0, 0.0, before)
        at = start - low
        cot3[row, f, start:start + size, b * 128:(b + 1) * 128] = after[at:at + size].astype(BF)
        cot3[row, f, start:start + size, 768 + b * 128:768 + (b + 1) * 128] = before[at:at + size].astype(BF)


def block_kernel(lat_hbm, cot_hbm, tw_hbm, sw_hbm, lg_hbm, tg_hbm, sg_hbm,
                 lat, cot3, back, hid, pgx, tw, twt, sw, part, out, lg,
                 in_sem, w_sem, l_sem, u_sem, d_sem, p_sem, o_sem, relay, r_sem, *refs):
    place = Place()
    tm, height = place.tm, place.height
    cot_in = [pltpu.make_async_copy(cot_hbm.at[:, r], cot3.at[r + 1, :, :, 384:768], in_sem.at[r]) for r in range(2)]
    lat_in = pltpu.make_async_copy(lat_hbm, lat.at[2:4], in_sem.at[2])
    tw_in = pltpu.make_async_copy(tw_hbm, tw, in_sem.at[3])
    sw_in = [pltpu.make_async_copy(sw_hbm.at[i, j], sw.at[i, :, j * 384:(j + 1) * 384], w_sem.at[3 * i + j])
             for i in (1, 0, 2) for j in range(3)]
    twt_in = [pltpu.make_async_copy(tw_hbm.at[k], twt.at[:, k * 384:(k + 1) * 384], w_sem.at[9 + k]) for k in range(3)]
    for copy in cot_in + sw_in + [lat_in, tw_in] + twt_in:
        copy.start()

    greet(place, True)

    def l_copy(c):
        cols = pl.ds(c * CW, CW)
        return remote(lat_hbm.at[:, :, cols], lat.at[0:2, :, cols], l_sem.at[c, 0], l_sem.at[c, 1],
                      ((tm + 1) % 4, height))

    def columns(c):
        return pl.ds(BOUNDS[c], BOUNDS[c + 1] - BOUNDS[c])

    def down_copy(c, f):
        cols = columns(c)
        return remote(cot_hbm.at[f, 1, cols], cot3.at[0, f, cols, 384:768], d_sem.at[c, f, 0], d_sem.at[c, f, 1],
                      (tm, (height + 1) % 32))

    def up_copy(c, f):
        cols = columns(c)
        return remote(cot_hbm.at[f, 0, cols], cot3.at[3, f, cols, 384:768], u_sem.at[c, f, 0], u_sem.at[c, f, 1],
                      (tm, (height + 31) % 32))

    x, y, z = place.xyz

    def slot(way, c, f):
        return relay.at[way, f, 0:BOUNDS[c + 1] - BOUNDS[c]]

    def to_relay(way, c, f):
        sem = (d_sem, u_sem)[way]
        device = (place.mirror, place.opposite, place.at(3 - x, y, z, place.core), place.at(x, y, 3 - z, place.core))[c]
        return remote(cot_hbm.at[f, 1 - way, columns(c)], slot(way, c, f), sem.at[c, f, 0], r_sem.at[way, f, 1], device)

    def to_mirror(way, c, f):
        return remote(slot(way, c, f), slot(way, c, f), r_sem.at[way, f, 0], r_sem.at[way, f, 1], place.mirror)

    def to_band(way, c, f):
        sem, row = ((d_sem, 0), (u_sem, 3))[way]
        device = (place.opposite, place.mirror, place.at(x, y, 3 - z, place.core), place.at(3 - x, y, z, place.core))[c]
        return remote(slot(way, c, f), cot3.at[row, f, columns(c), 384:768], r_sem.at[way, f, 0], sem.at[c, f, 1], device)

    def here(way, c):
        own = 3 - 3 * way
        column = ((x == own) & (z == own), (x == 3 - own) & (z == 3 - own), (x == 3 - own) & (z == own),
                  (x == own) & (z == 3 - own))[c]
        return place.corner & column

    def forward_first(f):
        for way in range(2):
            for c in range(1, 4):
                @pl.when(here(way, c) & (place.half == way))
                def _():
                    to_mirror(way, c, f).wait_recv()
                    (to_band if c == 1 else to_mirror)(way, c, f).start()

    def forward_second(f):
        for way in range(2):
            for c in (0, 2, 3):
                @pl.when(here(way, c) & (place.half == 1 - way))
                def _():
                    to_mirror(way, c, f).wait_recv()
                    to_band(way, c, f).start()

    def forward_sends(f):
        for way in range(2):
            for c in range(4):
                @pl.when(here(way, c) & (place.half == (1 - way if c == 0 else way)))
                def _():
                    to_mirror(way, c, f).wait_send()

            for c in (2, 3):
                @pl.when(here(way, c) & (place.half == 1 - way))
                def _():
                    to_mirror(way, c, f).wait_send()

    def p_copy(c):
        cols = pl.ds(c * CW, CW)
        return remote(pgx.at[0:2, :, cols], pgx.at[2:4, :, cols], p_sem.at[c, 0], p_sem.at[c, 1],
                      ((tm + 3) % 4, height))

    for c in range(CHUNKS):
        for f in range(2):
            @pl.when(height == 15)
            def _():
                to_relay(0, c, f).start()

            @pl.when(height == 16)
            def _():
                to_relay(1, c, f).start()

            @pl.when((height < 31) & (height != 15))
            def _():
                down_copy(c, f).start()

            @pl.when((height > 0) & (height != 16))
            def _():
                up_copy(c, f).start()

        @pl.when(tm < 3)
        def _():
            l_copy(c).start()

    @pl.when(tm == 0)
    def _():
        lat[0:2] = jnp.zeros((2, 2, 640, 384), BF)

    @pl.when(tm == 3)
    def _():
        pgx[2:4] = jnp.zeros((2, 2, 640, 384), BF)

    @pl.when(height == 0)
    def _():
        cot3[0, :, :, 384:768] = jnp.zeros((2, 640, 384), BF)

    @pl.when(height == 31)
    def _():
        cot3[3, :, :, 384:768] = jnp.zeros((2, 640, 384), BF)

    for copy in cot_in:
        copy.wait()
    for row in (1, 2):
        for f in range(2):
            shifts(cot3, row, f, 0, 640)
    for copy in sw_in:
        copy.wait()
    for f in range(2):
        back[0, f] = nt(lanes(cot3[1, f], cot3[2, f]), lanes(sw[1], sw[0]))
        forward_first(f)
        back[1, f] = nt(lanes(cot3[2, f], cot3[1, f]), lanes(sw[1], sw[2]))
    lat_in.wait()
    tw_in.wait()
    for copy in twt_in:
        copy.wait()

    def add(g, lanes_of, half, value):
        part[g, :, lanes_of] = value if half == 0 else part[g, :, lanes_of] + value

    def spatial(i, half):
        cols = slice(half * 320, (half + 1) * 320)
        value = tn(hid[:, :, cols].reshape(1280, 384), cot3[2 - i:4 - i, :, cols].reshape(1280, 1152))
        add(i, slice(0, 1152), half, value)

    def temporal(half):
        cols = slice(half * 320, (half + 1) * 320)
        grads = pgx[0:2, :, cols].reshape(1280, 384)
        for k in range(3):
            value = tn(lat[2 - k:4 - k, :, cols].reshape(1280, 384), grads)
            add(3, slice(k * 384, (k + 1) * 384), half, value)

    weight = tw.reshape(1152, 384)
    def forward_part(c):
        cols = slice(c * CW, (c + 1) * CW)

        @pl.when(tm > 0)
        def _():
            l_copy(c).wait_recv()

        factors = []
        for r in range(2):
            left = jnp.concatenate(
                [lanes(lat[f + 2, r, cols], lat[f + 1, r, cols], lat[f, r, cols]) for f in range(2)], axis=0)
            pre = jnp.dot(left, weight[...], preferred_element_type=F32)
            sigma = jax.nn.sigmoid(pre)
            hidden = (pre * sigma).astype(BF)
            for f in range(2):
                hid[r, f, cols] = hidden[f * CW:(f + 1) * CW]
            factors.append(sigma * (1.0 + pre * (1.0 - sigma)))
        return factors

    def backward_part(c, factors):
        cols = slice(c * CW, (c + 1) * CW)
        for f in range(2):
            @pl.when(height > 0)
            def _():
                down_copy(c, f).wait_recv()

            @pl.when(height < 31)
            def _():
                up_copy(c, f).wait_recv()

        for row in (0, 3):
            for f in range(2):
                shifts(cot3, row, f, c * CW, CW)
        for r in range(2):
            halo, i = (0, 2) if r == 0 else (3, 0)
            window = jnp.concatenate([cot3[halo, f, cols] for f in range(2)], axis=0)
            total = nt(window, sw[i]) + jnp.concatenate([back[r, f, cols] for f in range(2)], axis=0)
            grad = (total * factors[r]).astype(BF)
            for f in range(2):
                pgx[f, r, cols] = grad[f * CW:(f + 1) * CW]

        @pl.when(tm > 0)
        def _():
            p_copy(c).start()

    red = Reduce(place, part, out, refs)
    factors = [forward_part(0)]
    forward_second(0)
    factors.append(forward_part(1))
    spatial(1, 0)
    forward_second(1)
    for c in (0, 1):
        backward_part(c, factors[c])
    spatial(0, 0)
    spatial(2, 0)
    temporal(0)
    factors = [forward_part(c) for c in (2, 3)]
    spatial(1, 1)
    red.step0(1)
    for c in (2, 3):
        backward_part(c, factors[c - 2])

    def latent(f, r):
        grads = lanes(*(pgx[f + k, r] for k in range(3)))
        lg[f, r] = (cot3[r + 1, f, :, 384:768].astype(F32) + nt(grads, twt[...])).astype(BF)
        pltpu.make_async_copy(lg.at[f, r], lg_hbm.at[f, r], o_sem.at[4 + 2 * f + r]).start()

    def store(g):
        target = sg_hbm.at[g] if g < 3 else tg_hbm
        return pltpu.make_async_copy(out.at[3 * g:3 * g + 3], target, o_sem.at[g])

    def arrive():
        for c in range(CHUNKS):
            @pl.when(tm < 3)
            def _():
                p_copy(c).wait_recv()

    def last(g):
        red.step7(g)
        store(g).start()

    spatial(0, 1)
    red.step0(0)
    red.step1(1)
    spatial(2, 1)
    red.step0(2)
    red.step1(0)
    temporal(1)
    red.step1(2)
    red.step0(3)
    red.step2(0)
    red.step2(1)
    red.step1(3)
    red.step2(2)
    red.step2(3)
    red.step3(0)
    red.step3(1)
    red.step3(2)
    red.step3(3)
    red.step4(0)
    red.step4(1)
    red.step4(2)
    red.step4(3)
    red.step5(0)
    red.step5(1)
    red.step5(2)
    red.step5(3)
    arrive()
    latent(0, 0)
    latent(0, 1)
    latent(1, 0)
    red.step6(0)
    red.step6(1)
    red.step6(2)
    red.step6(3)
    latent(1, 1)
    last(0)
    last(1)
    last(2)
    last(3)

    for c in range(CHUNKS):
        @pl.when(tm < 3)
        def _():
            l_copy(c).wait_send()

        for f in range(2):
            @pl.when(height < 31)
            def _():
                down_copy(c, f).wait_send()

            @pl.when(height > 0)
            def _():
                up_copy(c, f).wait_send()

        @pl.when(tm > 0)
        def _():
            p_copy(c).wait_send()
    for f in range(2):
        forward_sends(f)
    for g in range(4):
        red.sends(g)
        store(g).wait()
    for f in range(2):
        for r in range(2):
            pltpu.make_async_copy(lg.at[f, r], lg_hbm.at[f, r], o_sem.at[4 + 2 * f + r]).wait()


def scale_kernel(scale, lg_ref, tg_ref, sg_ref, lg_out, tg_out, sg_out):
    lg_out[...] = lg_ref[...]
    tg_out[...] = tg_ref[...].astype(F32) * scale
    sg_out[...] = sg_ref[...].astype(F32) * scale


def scaled(latent_grad, temporal, spatial, scale):
    def blocks(rows):
        return pl.BlockSpec((rows // 8, 384), lambda i: (i, 0))

    latent_grad, temporal, spatial = pl.pallas_call(
        functools.partial(scale_kernel, scale),
        grid=(8,),
        out_shape=(
            jax.ShapeDtypeStruct((2560, 384), BF),
            jax.ShapeDtypeStruct((1152, 384), F32),
            jax.ShapeDtypeStruct((3456, 384), F32),
        ),
        in_specs=[blocks(2560), blocks(1152), blocks(3456)],
        out_specs=(blocks(2560), blocks(1152), blocks(3456)),
        compiler_params=pltpu.CompilerParams(vmem_limit_bytes=60 * 2**20),
    )(latent_grad.reshape(2560, 384), temporal.reshape(1152, 384), spatial.reshape(3456, 384))
    return latent_grad.reshape(2, 2, 640, 384), temporal.reshape(3, 384, 384), spatial.reshape(3, 3, 384, 384)


def on_device(latents, cotangent, temporal_weight, spatial_weight):
    frames, rows, cols, chans = latents.shape
    count = frames * lax.axis_size("tm") * rows * lax.axis_size("height") * cols
    scale = 1.0 / math.sqrt(count)
    anywhere = pl.BlockSpec(memory_space=pl.ANY)
    latent_grad, temporal, spatial = pl.pallas_call(
        block_kernel,
        out_shape=(
            jax.ShapeDtypeStruct((2, 2, 640, 384), BF),
            jax.ShapeDtypeStruct((3, 384, 384), BF),
            jax.ShapeDtypeStruct((3, 3, 384, 384), BF),
        ),
        in_specs=[anywhere] * 4,
        out_specs=(anywhere,) * 3,
        scratch_shapes=[
            pltpu.VMEM((4, 2, 640, 384), BF),
            pltpu.VMEM((4, 2, 640, 1152), BF),
            pltpu.VMEM((2, 2, 640, 384), F32),
            pltpu.VMEM((2, 2, 640, 384), BF),
            pltpu.VMEM((4, 2, 640, 384), BF),
            pltpu.VMEM((3, 384, 384), BF),
            pltpu.VMEM((384, 1152), BF),
            pltpu.VMEM((3, 384, 1152), BF),
            pltpu.VMEM((4, 384, 1152), F32),
            pltpu.VMEM((12, 384, 384), BF),
            pltpu.VMEM((2, 2, 640, 384), BF),
            pltpu.SemaphoreType.DMA((4,)),
            pltpu.SemaphoreType.DMA((12,)),
            pltpu.SemaphoreType.DMA((CHUNKS, 2)),
            pltpu.SemaphoreType.DMA((CHUNKS, 2, 2)),
            pltpu.SemaphoreType.DMA((CHUNKS, 2, 2)),
            pltpu.SemaphoreType.DMA((CHUNKS, 2)),
            pltpu.SemaphoreType.DMA((8,)),
            pltpu.VMEM((2, 2, 176, 384), BF),
            pltpu.SemaphoreType.DMA((2, 2, 2)),
        ] + Reduce.SCRATCH,
        compiler_params=pltpu.CompilerParams(
            collective_id=0, has_side_effects=True, vmem_limit_bytes=60 * 2**20),
    )(latents, cotangent, temporal_weight, spatial_weight)
    return scaled(latent_grad, temporal, spatial, scale)


def solution(mesh):
    return jax.shard_map(
        on_device,
        mesh=mesh,
        in_specs=(P("tm", "height", None, None), P("tm", "height", None, None), P(), P()),
        out_specs=(P("tm", "height", None, None), P(), P()),
        check_vma=False,
    )
```
